32 devices in a mesh: row: 4 (over z), col: 8 (over y, x, core).
Axes of the slice: x: 2, y: 2, z: 4, core: 2. Of those that a mesh axis runs over, the one named last changes fastest.
Arguments:
- panel: float32 [4, 1536, 1, 8, 1536], P(None, 'row', None, 'col'), may hold values from -1 to 1, as said below
- inverse_blocks: float32 [4, 1536, 1536], P(None, 'row'), may hold values from -1 to 2, as said below
- right_side: float32 [48, 1, 8, 1536], P(None, None, 'col'), may hold values from -6 to 6
Outputs:
- solved: float32 [48, 4, 1536], P(None, None, 'row')
- updated: float32 [48, 1, 8, 1536], P(None, None, 'col', 'row')
The draws below stay inside these ranges and needn't reach their ends.
Inputs may be any that keep to these rules, and one draw needn't show every extreme that they name: panel is zero where the row index is below the column index as defined in its meaning (the factor is lower triangular). `inverse_blocks`: each inverse block is lower triangular with a positive diagonal.
All inputs are finite; a program needn't handle non-finite values.
Results may differ from the reference program's by a relative error of at most 0.0001.
Values sent between devices are 32-bit elements; how exact they have to be, the bound alone decides.
No kernel may reach another device: no remote copies, remote signals or barrier semaphores. Data moves between devices by JAX's collectives and lax.ppermute only.
A program may use at most 64 MiB of HBM per device.

```python
import jax
import jax.numpy as jnp
from jax import lax

B = 1536
K = 4
RHS = 48
NJ = 1
NC = 8


def draw_panel(key, part):
    shape = (K, B, NJ, NC, B)
    values = jnp.clip(jax.random.normal(key, shape, jnp.float32), -4.0, 4.0)
    values = values * (K * B) ** (-0.5)
    kidx = jnp.arange(K).reshape(K, 1, 1, 1, 1)
    cidx = jnp.arange(B).reshape(1, B, 1, 1, 1)
    jidx = jnp.arange(NJ).reshape(1, 1, NJ, 1, 1)
    qidx = jnp.arange(NC).reshape(1, 1, 1, NC, 1)
    iidx = jnp.arange(B).reshape(1, 1, 1, 1, B)
    row_at = (jidx * NC + qidx) * B + iidx
    col_at = kidx * B + cidx
    return jnp.where(row_at >= col_at, values, 0.0).astype(jnp.float32)


def draw_inverse_blocks(key, part):
    first = jax.random.fold_in(key, 11)
    second = jax.random.fold_in(key, 23)
    shape = (K, B, B)
    lower = jnp.clip(jax.random.normal(first, shape, jnp.float32), -4.0, 4.0)
    lower = lower * 0.5 * B ** (-0.5)
    diag_vals = jax.random.uniform(second, (K, B, 1), jnp.float32, 0.5, 1.5)
    ridx = jnp.arange(B).reshape(1, B, 1)
    cidx = jnp.arange(B).reshape(1, 1, B)
    result = jnp.where(cidx < ridx, lower, 0.0) + jnp.where(cidx == ridx, diag_vals, 0.0)
    return result.astype(jnp.float32)


def level_of(rng, extent, cuts, least, top_value):
    gain = 1.0
    for axis_at, shards_of in cuts:
        steps = jax.random.uniform(jax.random.fold_in(jax.random.fold_in(rng, 6), axis_at), (shards_of,), jnp.float32, least / len(cuts), top_value / len(cuts))
        gain = gain * jnp.repeat(jnp.exp(steps), extent[axis_at] // shards_of).reshape((-1,) + (1,) * (len(extent) - 1 - axis_at))
    return gain


def normal_values(rng, extent, width, bound, split=(), held_as=jnp.bfloat16):
    entries = width * jax.random.normal(rng, extent, jnp.float32)
    if split:
        entries = entries * level_of(rng, extent, split, -0.22, 0.18)
    return jnp.clip(entries, -bound, bound).astype(held_as)


def setup_inputs(seed: int = 0) -> dict:
    keys = jax.random.split(jax.random.key(seed), 4)
    panel = draw_panel(jax.random.fold_in(keys[3], 71), 0)
    inverse_blocks = draw_inverse_blocks(jax.random.fold_in(keys[3], 71), 0)
    right_side = normal_values(keys[2], (RHS, NJ, NC, B), 1.0, 6.0, ((2, 8),), jnp.float32)
    return {"panel": panel, "inverse_blocks": inverse_blocks, "right_side": right_side}


def reference(panel, inverse_blocks, right_side):
    solved_list = []
    for step in range(K):
        jblock = step // NC
        qblock = step % NC
        total = jnp.zeros((RHS, B), jnp.float32)
        for prior in range(step):
            total = total + jnp.dot(solved_list[prior], panel[prior, :, jblock, qblock, :], precision=lax.Precision.HIGHEST, preferred_element_type=jnp.float32)
        residue = right_side[:, jblock, qblock, :] - total
        solved_list.append(jnp.dot(residue, inverse_blocks[step].T, precision=lax.Precision.HIGHEST, preferred_element_type=jnp.float32))
    stacked = jnp.stack(solved_list, axis=1)
    trailing = jnp.zeros((RHS, NJ, NC, B), jnp.float32)
    for step in range(K):
        trailing = trailing + jnp.einsum("rc,cjqi->rjqi", stacked[:, step, :], panel[step], precision=lax.Precision.HIGHEST)
    return stacked, right_side - trailing
```

```python
import functools

import jax
import jax.numpy as jnp
from jax import lax
from jax.experimental import pallas as pl
from jax.experimental.pallas import tpu as pltpu
from jax.sharding import PartitionSpec as P

LANES = 128
F32 = jnp.float32
BF16 = jnp.bfloat16
VMEM = pl.BlockSpec(memory_space=pltpu.VMEM)
SMEM = pl.BlockSpec(memory_space=pltpu.SMEM)
PARAMS = pltpu.CompilerParams(vmem_limit_bytes=16 * 2**20)


def split(value):
    head = value.astype(BF16)
    return head, (value - head.astype(F32)).astype(BF16)


def product(left, right, dims):
    count = left.shape[0]
    left_head, left_tail = split(left)
    right_head, right_tail = split(right)
    dot = functools.partial(lax.dot_general, dimension_numbers=(dims, ((), ())), preferred_element_type=F32)
    stacked = dot(jnp.concatenate([left_head, left_tail], axis=0), right_head)
    return stacked[:count] + stacked[count:] + dot(left_head, right_tail)


def tile_columns(block_ref, index, width, rows, stride):
    first = index * width // LANES
    parts = [block_ref[pl.ds(first + at, rows, stride=stride), :] for at in range(width // LANES)]
    return parts[0] if len(parts) == 1 else jnp.concatenate(parts, axis=1)


def subtract_product(solved, base_ref, block_ref, out_ref):
    rows = solved.shape[1]
    length = base_ref.shape[1]
    stride = length // LANES
    width = 2 * LANES
    for index in range(length // width):
        at = slice(index * width, (index + 1) * width)
        tile = tile_columns(block_ref, index, width, rows, stride)
        out_ref[:, at] = base_ref[:, at] - product(solved, tile, ((1,), (0,)))


def update_kernel(solved_ref, base_ref, block_ref, out_ref):
    subtract_product(solved_ref[...], base_ref, block_ref, out_ref)


def update_either_kernel(own_ref, solved_ref, base_ref, block_ref, other_ref, out_ref):
    own = own_ref[0]

    @pl.when(own == 1)
    def _():
        subtract_product(solved_ref[...], base_ref, block_ref, out_ref)

    @pl.when(own != 1)
    def _():
        subtract_product(solved_ref[...], base_ref, other_ref, out_ref)


def apply_kernel(value_ref, inverse_ref, out_ref):
    out_ref[...] = product(value_ref[...], inverse_ref[0], ((1,), (1,)))


def gather_apply_kernel(fulls, flag_ref, own_ref, *refs):
    even = flag_ref[0]
    inverse_ref, out_ref = refs[-2:]
    half_refs = refs[fulls:-2]
    value = jnp.where(even == 1, own_ref[...], 0.0)
    for ref in refs[:fulls]:
        value = value + ref[...]
    if half_refs:
        half = half_refs[0][...]
        zero = jnp.zeros_like(half)
        value = value + jnp.concatenate([jnp.where(even == 1, half, zero), jnp.where(even == 1, zero, half)], axis=1)
    out_ref[...] = product(value, inverse_ref[0], ((1,), (1,)))


def cost(count, rows, columns):
    return pl.CostEstimate(flops=6 * count * rows * columns, bytes_accessed=4 * (rows * columns + count * (rows + columns)), transcendentals=0)


def update(solved, base, block):
    count, rows = solved.shape
    return pl.pallas_call(
        update_kernel,
        out_shape=jax.ShapeDtypeStruct(base.shape, F32),
        in_specs=[VMEM] * 3,
        out_specs=VMEM,
        compiler_params=PARAMS,
        cost_estimate=cost(count, rows, base.shape[1]),
    )(solved, base, block)


def update_either(own, solved, base, block, other):
    count, rows = solved.shape
    return pl.pallas_call(
        update_either_kernel,
        out_shape=jax.ShapeDtypeStruct(base.shape, F32),
        in_specs=[SMEM] + [VMEM] * 4,
        out_specs=VMEM,
        compiler_params=PARAMS,
        cost_estimate=cost(count, rows, base.shape[1]),
    )(own, solved, base, block, other)


def inverse_spec(inverse_blocks, step):
    return pl.BlockSpec((1,) + inverse_blocks.shape[1:], lambda *_: (step, 0, 0))


def whole(array):
    return pl.BlockSpec(array.shape, lambda *_: (0,) * array.ndim)


def apply(value, inverse_blocks, step):
    count, length = value.shape
    rows = inverse_blocks.shape[1]
    return pl.pallas_call(
        apply_kernel,
        grid=(1,),
        out_shape=jax.ShapeDtypeStruct((count, rows), F32),
        in_specs=[whole(value), inverse_spec(inverse_blocks, step)],
        out_specs=pl.BlockSpec((count, rows), lambda *_: (0, 0)),
        compiler_params=PARAMS,
        cost_estimate=cost(count, rows, length),
    )(value, inverse_blocks)


def gather_apply(even, own, fulls, halves, inverse_blocks, step):
    count, length = own.shape
    rows = inverse_blocks.shape[1]
    arrays = [own] + fulls + halves
    return pl.pallas_call(
        functools.partial(gather_apply_kernel, len(fulls)),
        grid=(1,),
        out_shape=jax.ShapeDtypeStruct((count, rows), F32),
        in_specs=[SMEM] + [whole(array) for array in arrays] + [inverse_spec(inverse_blocks, step)],
        out_specs=pl.BlockSpec((count, rows), lambda *_: (0, 0)),
        compiler_params=PARAMS,
        cost_estimate=cost(count, rows, length),
    )(even, *arrays, inverse_blocks)


def body(rows, cols, panel, inverse_blocks, right_side):
    steps, depth, _, _, length = panel.shape
    count = right_side.shape[0]
    row, col = lax.axis_index("row"), lax.axis_index("col")
    parity = lax.rem(col, 2)
    is_even = parity == 0
    even = jnp.where(is_even, 1, 0).astype(jnp.int32).reshape(1)
    odd = 1 - even

    def move(value, target):
        pairs = []
        for z in range(rows):
            for q in range(cols):
                to_z, to_q = target(z, q)
                pairs.append((z * cols + q, to_z * cols + to_q))
        return lax.ppermute(value, ("row", "col"), pairs)

    def swap_core(value):
        return move(value, lambda z, q: (z, q ^ 1))

    def spread(value, source, bits):
        for bit in bits:
            moved = move(value, lambda z, q: (z, q ^ bit))
            value = jnp.where(((col ^ source) & bit) != 0, moved, value)
        return value

    bits = [1 << at for at in range(1, cols.bit_length() - 1)]
    blocks = panel.reshape(steps, depth * length // LANES, LANES)
    block = [blocks[step] for step in range(steps)]
    other = [swap_core(block[step]) for step in range(steps - 1)]
    heads = right_side.reshape(count, length)
    accum = jnp.where(row == 0, heads, 0.0)

    offsets = list(range(1, rows))
    middle = offsets.pop(len(offsets) // 2) if offsets else 0
    first, second = offsets[0::2], offsets[1::2]

    def sum_apply(total, step):
        fulls, halves = [], []
        for m_even, m_odd in zip(first, second):
            fulls.append(move(total, lambda z, q: (z ^ (m_even if q % 2 == 0 else m_odd), q)))
        if middle:
            part = lax.dynamic_slice_in_dim(total, parity * (length // 2), length // 2, 1)
            halves.append(move(part, lambda z, q: (z ^ middle, q)))
        piece = gather_apply(even, total, fulls, halves, inverse_blocks, step)
        return piece + swap_core(piece)

    own_piece = apply(heads, inverse_blocks, 0)
    piece = jnp.where(is_even, own_piece, swap_core(own_piece))
    solved = []
    for step in range(1, steps):
        hops = [bit for bit in bits if ((step - 1) ^ step) & bit]
        piece = spread(piece, step - 1, hops)
        active_even = step % 2 == 0
        base = jnp.where(is_even if active_even else ~is_even, accum, swap_core(accum))
        total = update_either(even if active_even else odd, piece, base, block[step - 1], other[step - 1])
        solved.append(spread(piece, step - 1, [bit for bit in bits if bit not in hops]))
        accum = update(solved[-1], accum, block[step - 1])
        piece = sum_apply(total, step)
    solved.append(spread(piece, steps - 1, bits))
    accum = update(solved[-1], accum, block[steps - 1])

    size = length // rows
    chunk = lambda at: lax.dynamic_slice_in_dim(accum, at * size, size, 1)
    updated = chunk(row)
    for offset in range(rows - 1, 0, -1):
        updated = updated + move(chunk(row ^ offset), lambda z, q: (z ^ offset, q))
    return jnp.stack(solved, axis=1), updated[:, None, None, :]


def solution(mesh):
    placed = (P(None, "row", None, "col", None), P(None, "row", None), P(None, None, "col", None))
    return jax.shard_map(
        functools.partial(body, mesh.shape["row"], mesh.shape["col"]),
        mesh=mesh,
        in_specs=placed,
        out_specs=(P(None, None, "row"), P(None, None, "col", "row")),
        check_vma=False,
    )
```

```python
import functools

import jax
import jax.numpy as jnp
from jax import lax
from jax.experimental import pallas as pl
from jax.experimental.pallas import tpu as pltpu
from jax.sharding import PartitionSpec as P

LANES = 128
F32 = jnp.float32
BF16 = jnp.bfloat16
VMEM = pl.BlockSpec(memory_space=pltpu.VMEM)
SMEM = pl.BlockSpec(memory_space=pltpu.SMEM)
ANY = pl.BlockSpec(memory_space=pl.ANY)
HBM = pl.BlockSpec(memory_space=pltpu.HBM)
PARAMS = pltpu.CompilerParams(vmem_limit_bytes=8 * 2**20)


def split(value):
    head = value.astype(BF16)
    return head, (value - head.astype(F32)).astype(BF16)


def product(left, right, dims):
    count = left.shape[0]
    left_head, left_tail = split(left)
    right_head, right_tail = split(right)
    dot = functools.partial(lax.dot_general, dimension_numbers=(dims, ((), ())), preferred_element_type=F32)
    stacked = dot(jnp.concatenate([left_head, left_tail], axis=0), right_head)
    return stacked[:count] + stacked[count:] + dot(left_head, right_tail)


def columns(block_ref, first, width, rows):
    if block_ref.shape[0] == rows:
        return block_ref[:, first : first + width]
    stride = block_ref.shape[0] // rows
    parts = [block_ref[pl.ds(at // LANES, rows, stride=stride), :] for at in range(first, first + width, LANES)]
    return parts[0] if len(parts) == 1 else jnp.concatenate(parts, axis=1)


def subtract_products(solved, base_ref, block_refs, out_ref):
    length = base_ref.shape[1]
    width = 2 * LANES
    for first in range(0, length, width):
        at = slice(first, first + width)
        total = base_ref[:, at]
        for value, block_ref in zip(solved, block_refs):
            total = total - product(value, columns(block_ref, first, width, value.shape[1]), ((1,), (0,)))
        out_ref[:, at] = total


def call(kernel, outs, ins, in_specs, flops=0, scratch=()):
    moved = sum(4 * out.size for out in outs) if flops else 0
    return pl.pallas_call(
        kernel,
        out_shape=outs,
        in_specs=in_specs,
        out_specs=[VMEM] * len(outs),
        scratch_shapes=scratch,
        compiler_params=PARAMS,
        cost_estimate=pl.CostEstimate(flops=flops, bytes_accessed=moved, transcendentals=0),
    )(*ins)


def shape(*sizes):
    return jax.ShapeDtypeStruct(sizes, F32)


def start(copies):
    for copy in copies:
        copy.start()


def finish(copies):
    for copy in copies:
        copy.wait()


def first_step(keep, heads, inverse_blocks, count):
    rows, length = inverse_blocks.shape[1:]
    stride = heads.shape[0] // count
    pieces = 3 if rows % (3 * LANES) == 0 else 1
    size = rows // pieces

    def kernel(keep_ref, heads_ref, inverse_ref, out_ref, kept_ref, heads_here, inverse_here, sems):
        copies = [pltpu.make_async_copy(heads_ref, heads_here, sems.at[pieces])]
        for at in range(pieces):
            piece = pl.ds(at * size, size)
            copies.append(pltpu.make_async_copy(inverse_ref.at[0, piece], inverse_here.at[piece], sems.at[at]))
        start(copies)
        copies[0].wait()
        value = columns(heads_here, 0, stride * LANES, count)
        kept_ref[...] = jnp.where(keep_ref[0] == 1, value, 0.0)
        for at in range(pieces):
            piece = slice(at * size, (at + 1) * size)
            copies[at + 1].wait()
            out_ref[:, piece] = product(value, inverse_here[piece, :], ((1,), (1,)))

    return call(
        kernel,
        [shape(count, rows), shape(count, length)],
        [keep, heads, inverse_blocks],
        [SMEM, HBM, HBM],
        6 * count * rows * length,
        [pltpu.VMEM(heads.shape, F32), pltpu.VMEM((rows, length), F32), pltpu.SemaphoreType.DMA((pieces + 1,))],
    )


def after(token, value):
    def kernel(token_ref, value_ref, out_ref):
        out_ref[...] = value_ref[...]

    return call(kernel, [shape(*value.shape)], [token, value], [ANY, VMEM])[0]


def load(token, arrays):
    wanted = [(at, index) for at, (_, indices) in enumerate(arrays) for index in indices]

    def kernel(token_ref, *refs):
        ins, outs, sems = refs[: len(arrays)], refs[len(arrays) : -1], refs[-1]
        copies = [
            pltpu.make_async_copy(ins[at].at[index], out, sems.at[n]) for n, ((at, index), out) in enumerate(zip(wanted, outs))
        ]
        start(copies)
        finish(copies)

    return call(
        kernel,
        [shape(*arrays[at][0].shape[1:]) for at, _ in wanted],
        [token] + [array for array, _ in arrays],
        [ANY] + [HBM] * len(arrays),
        scratch=[pltpu.SemaphoreType.DMA((len(wanted),))],
    )


def update(solved, base, blocks, urgent=True):
    many = len(solved)

    def kernel(*refs):
        subtract_products([ref[...] for ref in refs[:many]], refs[many], refs[many + 1 : -1], refs[-1])

    flops = 6 * base.size * sum(value.shape[1] for value in solved) if urgent else 0
    ins = list(solved) + [base] + list(blocks)
    return call(kernel, [shape(*base.shape)], ins, [VMEM] * len(ins), flops)[0]


def gather_apply(odd, own, fulls, halves, inverse):
    count, length = own.shape
    rows = inverse.shape[0]

    def kernel(odd_ref, *refs):
        odd = odd_ref[0]
        own_ref, rest = refs[0], refs[1:-2]
        inverse_ref, out_ref = refs[-2:]
        value = jnp.where(odd == 1, 0.0, own_ref[...])
        for ref in rest[: len(fulls)]:
            value = value + ref[...]
        for ref in rest[len(fulls) :]:
            half = ref[...]
            zero = jnp.zeros_like(half)
            value = value + jnp.concatenate([jnp.where(odd == 1, zero, half), jnp.where(odd == 1, half, zero)], axis=1)
        out_ref[...] = product(value, inverse_ref[...], ((1,), (1,)))

    ins = [own] + fulls + halves + [inverse]
    return call(kernel, [shape(count, rows)], [odd.reshape(1)] + ins, [SMEM] + [VMEM] * len(ins), 6 * own.size * rows)[0]


def body(rows, cols, panel, inverse_blocks, right_side):
    steps, depth, _, _, length = panel.shape
    count = right_side.shape[0]
    row, col = lax.axis_index("row"), lax.axis_index("col")
    odd = lax.rem(col, 2)
    is_odd, is_right = odd == 1, lax.rem(col // 2, 2) == 1
    bits = [1 << at for at in range(1, cols.bit_length() - 1)]

    def move(value, target, senders=range(cols)):
        pairs = []
        for z in range(rows):
            for q in senders:
                to_z, to_q = target(z, q)
                pairs.append((z * cols + q, to_z * cols + to_q))
        return lax.ppermute(value, ("row", "col"), pairs)

    def swap_core(value):
        return move(value, lambda z, q: (z, q ^ 1))

    def spread(value, source, bits):
        for bit in bits:
            moved = move(value, lambda z, q: (z, q ^ bit))
            value = jnp.where(((col ^ source) & bit) != 0, moved, value)
        return value

    offsets = list(range(1, rows))
    middle = offsets.pop(len(offsets) // 2) if offsets else 0
    first, second = offsets[0::2], offsets[1::2]

    def sum_apply(total, part, inverse):
        fulls = [move(total, lambda z, q: (z ^ (b if q % 2 else a), q)) for a, b in zip(first, second)]
        halves = [move(part, lambda z, q: (z ^ middle, q))] if middle else []
        piece = gather_apply(odd, total, fulls, halves, inverse)
        return piece + swap_core(piece)

    half = length // 2
    blocks = panel.reshape(steps, depth * length // LANES, LANES)
    blocks = pltpu.with_memory_space_constraint(blocks, pltpu.HBM)
    inverse_blocks = pltpu.with_memory_space_constraint(inverse_blocks, pltpu.HBM)
    heads = pltpu.with_memory_space_constraint(right_side.reshape(count * length // LANES, LANES), pltpu.HBM)

    def to_right(value):
        return jnp.where(is_right, move(value, lambda z, q: (z, q ^ 2), (0, 1)), value)

    keep = jnp.where(row == 0, 1, 0).astype(jnp.int32).reshape(1)
    own_piece, start_value = first_step(keep, heads, inverse_blocks, count)
    x_0 = jnp.where(is_odd, swap_core(own_piece), own_piece)
    (block_0,) = load(own_piece, [(blocks, (0,))])

    def on_chip(total, step):
        total = jnp.where(is_odd == (step % 2 == 1), total, swap_core(total))
        return total, lax.dynamic_slice_in_dim(total, odd * half, half, 1)

    own_total = update([x_0], start_value, [block_0])
    total, part = on_chip(own_total, 1)
    inverse_1, block_1 = load(total, [(inverse_blocks, (1,)), (blocks, (1,))])
    x_0 = to_right(after(total, x_0))
    early = update([x_0], start_value, [block_0], False)
    x_1 = to_right(sum_apply(total, part, inverse_1))

    own_total = update([x_1], early, [block_1])
    total, part = on_chip(own_total, 2)
    inverse_2, block_2 = load(total, [(inverse_blocks, (2,)), (blocks, (2,))])
    x_2 = sum_apply(total, part, inverse_2)

    own_total = update([x_2], own_total, [block_2])
    total, part = on_chip(own_total, 3)
    inverse_3, block_3 = load(total, [(inverse_blocks, (3,)), (blocks, (3,))])
    x_2 = spread(after(total, x_2), 2, bits[:1])
    before = spread(jnp.concatenate([x_0, x_1, x_2], axis=1), 2, bits[1:])
    before = [before[:, at * depth : (at + 1) * depth] for at in range(3)]
    accum = update(before, start_value, [block_0, block_1, block_2], False)
    x_3 = spread(sum_apply(total, part, inverse_3), 2, bits)
    accum = update([x_3], accum, [block_3])

    size = length // rows
    chunk = lambda at: lax.dynamic_slice_in_dim(accum, at * size, size, 1)
    updated = chunk(row)
    for offset in range(rows - 1, 0, -1):
        updated = updated + move(chunk(row ^ offset), lambda z, q: (z ^ offset, q))
    return jnp.stack(before + [x_3], axis=1), updated[:, None, None, :]


def solution(mesh):
    placed = (P(None, "row", None, "col", None), P(None, "row", None), P(None, None, "col", None))
    return jax.shard_map(
        functools.partial(body, mesh.shape["row"], mesh.shape["col"]),
        mesh=mesh,
        in_specs=placed,
        out_specs=(P(None, None, "row"), P(None, None, "col", "row")),
        check_vma=False,
    )
```

```python
import functools

import jax
import jax.numpy as jnp
from jax import lax
from jax.experimental import pallas as pl
from jax.experimental.pallas import tpu as pltpu
from jax.sharding import PartitionSpec as P

LANES = 128
F32 = jnp.float32
BF16 = jnp.bfloat16
VMEM = pl.BlockSpec(memory_space=pltpu.VMEM)
SMEM = pl.BlockSpec(memory_space=pltpu.SMEM)
ANY = pl.BlockSpec(memory_space=pl.ANY)
HBM = pl.BlockSpec(memory_space=pltpu.HBM)
PARAMS = pltpu.CompilerParams(vmem_limit_bytes=12 * 2**20)


def split(value):
    head = value.astype(BF16)
    return head, (value - head.astype(F32)).astype(BF16)


def product(left, right, dims):
    count = left.shape[0]
    left_head, left_tail = split(left)
    right_head, right_tail = split(right)
    dot = functools.partial(lax.dot_general, dimension_numbers=(dims, ((), ())), preferred_element_type=F32)
    stacked = dot(jnp.concatenate([left_head, left_tail], axis=0), right_head)
    return stacked[:count] + stacked[count:] + dot(left_head, right_tail)


def columns(block_ref, first, width, rows):
    if block_ref.shape[0] == rows:
        return block_ref[:, first : first + width]
    stride = block_ref.shape[0] // rows
    parts = [block_ref[pl.ds(at // LANES, rows, stride=stride), :] for at in range(first, first + width, LANES)]
    return parts[0] if len(parts) == 1 else jnp.concatenate(parts, axis=1)


def subtract_products(solved, base_ref, block_refs, out_ref):
    length = base_ref.shape[1]
    width = 2 * LANES
    for first in range(0, length, width):
        at = slice(first, first + width)
        total = base_ref[:, at]
        for value, block_ref in zip(solved, block_refs):
            total = total - product(value, columns(block_ref, first, width, value.shape[1]), ((1,), (0,)))
        out_ref[:, at] = total


def call(kernel, outs, ins, in_specs, flops=0, scratch=()):
    moved = sum(4 * out.size for out in outs) if flops else 0
    return pl.pallas_call(
        kernel,
        out_shape=outs,
        in_specs=in_specs,
        out_specs=[VMEM] * len(outs),
        scratch_shapes=scratch,
        compiler_params=PARAMS,
        cost_estimate=pl.CostEstimate(flops=flops, bytes_accessed=moved, transcendentals=0),
    )(*ins)


def shape(*sizes):
    return jax.ShapeDtypeStruct(sizes, F32)


def start(copies):
    for copy in copies:
        copy.start()


def finish(copies):
    for copy in copies:
        copy.wait()


def first_step(keep, heads, inverse_blocks, blocks, count):
    rows, length = inverse_blocks.shape[1:]
    stride = heads.shape[0] // count
    pieces = 3
    size = length // pieces

    def kernel(keep_ref, heads_ref, inverse_ref, blocks_ref, out_ref, kept_ref, block_ref, heads_here, inverse_here, sems):
        copies = [pltpu.make_async_copy(heads_ref, heads_here, sems.at[pieces])]
        for at in range(pieces):
            piece = pl.ds(at * size, size)
            copies.append(pltpu.make_async_copy(inverse_ref.at[0, :, piece], inverse_here.at[:, piece], sems.at[at]))
        later = chunked(blocks_ref.at[0], block_ref, sems, pieces + 1)
        start(copies + later)
        copies[0].wait()
        value = columns(heads_here, 0, stride * LANES, count)
        kept_ref[...] = jnp.where(keep_ref[0] == 1, value, 0.0)
        total = jnp.zeros((count, rows), F32)
        for at in range(pieces):
            piece = slice(at * size, (at + 1) * size)
            copies[at + 1].wait()
            total = total + product(value[:, piece], inverse_here[:, piece], ((1,), (1,)))
        out_ref[...] = total
        finish(later)

    return call(
        kernel,
        [shape(count, rows), shape(count, length), shape(*blocks.shape[1:])],
        [keep, heads, inverse_blocks, blocks],
        [SMEM, HBM, HBM, HBM],
        6 * count * rows * length,
        [pltpu.VMEM(heads.shape, F32), pltpu.VMEM((rows, length), F32), pltpu.SemaphoreType.DMA((pieces + 5,))],
    )


def after(token, value):
    def kernel(token_ref, value_ref, out_ref):
        out_ref[...] = value_ref[...]

    return call(kernel, [shape(*value.shape)], [token, value], [ANY, VMEM])[0]


def chunked(source, target, sems, first, pieces=4):
    size = target.shape[0] // pieces
    parts = [pl.ds(at * size, size) for at in range(pieces)]
    return [pltpu.make_async_copy(source.at[part], target.at[part], sems.at[first + at]) for at, part in enumerate(parts)]


def load(token, arrays):
    wanted = [(at, index) for at, (_, indices) in enumerate(arrays) for index in indices]

    def kernel(token_ref, *refs):
        ins, outs, sems = refs[: len(arrays)], refs[len(arrays) : -1], refs[-1]
        copies = []
        for (at, index), out in zip(wanted, outs):
            copies += chunked(ins[at].at[index], out, sems, len(copies))
        start(copies)
        finish(copies)

    return call(
        kernel,
        [shape(*arrays[at][0].shape[1:]) for at, _ in wanted],
        [token] + [array for array, _ in arrays],
        [ANY] + [HBM] * len(arrays),
        scratch=[pltpu.SemaphoreType.DMA((4 * len(wanted),))],
    )


def update_from(token, solved, base, blocks, indices):
    many = len(solved)

    def kernel(*refs):
        solved_refs, base_ref, blocks_ref, _, out_ref, here, sems = refs[:many], *refs[many:]
        copies = [chunked(blocks_ref.at[index], here.at[at], sems, 4 * at) for at, index in enumerate(indices)]
        for copy in copies:
            start(copy)
        for copy in copies:
            finish(copy)
        subtract_products([ref[...] for ref in solved_refs], base_ref, [here.at[at] for at in range(many)], out_ref)

    return call(
        kernel,
        [shape(*base.shape)],
        list(solved) + [base, blocks, token],
        [VMEM] * (many + 1) + [HBM, ANY],
        scratch=[pltpu.VMEM((many,) + blocks.shape[1:], F32), pltpu.SemaphoreType.DMA((4 * many,))],
    )[0]


def update(solved, base, blocks):
    many = len(solved)

    def kernel(*refs):
        subtract_products([ref[...] for ref in refs[:many]], refs[many], refs[many + 1 : -1], refs[-1])

    flops = 6 * base.size * sum(value.shape[1] for value in solved)
    ins = list(solved) + [base] + list(blocks)
    return call(kernel, [shape(*base.shape)], ins, [VMEM] * len(ins), flops)[0]


def add_rows(parts):
    count, length = parts[0].shape
    many = length // LANES
    if many * LANES != length:
        return sum(parts)

    def kernel(*refs):
        total = refs[0][...]
        for ref in refs[1:-1]:
            total = total + ref[...]
        for at in range(many):
            refs[-1][pl.ds(at, count, stride=many), :] = total[:, at * LANES : (at + 1) * LANES]

    return call(kernel, [shape(count * many, LANES)], parts, [VMEM] * len(parts), parts[0].size)[0]


def gather_apply(odd, own, fulls, halves, inverse, hold):
    count, length = own.shape
    rows = inverse.shape[0]

    def kernel(odd_ref, *refs):
        odd = odd_ref[0]
        own_ref, rest = refs[0], refs[1 : -2 - len(hold)]
        inverse_ref, out_ref = refs[-2 - len(hold)], refs[-1]
        value = jnp.where(odd == 1, 0.0, own_ref[...])
        for ref in rest[: len(fulls)]:
            value = value + ref[...]
        for ref in rest[len(fulls) :]:
            half = ref[...]
            zero = jnp.zeros_like(half)
            value = value + jnp.concatenate([jnp.where(odd == 1, zero, half), jnp.where(odd == 1, half, zero)], axis=1)
        out_ref[...] = product(value, inverse_ref[...], ((1,), (1,)))

    ins = [own] + fulls + halves + [inverse]
    specs = [SMEM] + [VMEM] * len(ins) + [ANY] * len(hold)
    return call(kernel, [shape(count, rows)], [odd.reshape(1)] + ins + hold, specs, 6 * own.size * rows)[0]


def body(rows, cols, panel, inverse_blocks, right_side):
    steps, depth, _, _, length = panel.shape
    count = right_side.shape[0]
    row, col = lax.axis_index("row"), lax.axis_index("col")
    odd = lax.rem(col, 2)
    is_odd, is_right = odd == 1, lax.rem(col // 2, 2) == 1
    bits = [1 << at for at in range(1, cols.bit_length() - 1)]

    def move(value, target, senders=range(cols)):
        pairs = []
        for z in range(rows):
            for q in senders:
                to_z, to_q = target(z, q)
                pairs.append((z * cols + q, to_z * cols + to_q))
        return lax.ppermute(value, ("row", "col"), pairs)

    def swap_core(value):
        return move(value, lambda z, q: (z, q ^ 1))

    def spread(value, source, bits):
        for bit in bits:
            moved = move(value, lambda z, q: (z, q ^ bit))
            value = jnp.where(((col ^ source) & bit) != 0, moved, value)
        return value

    offsets = list(range(1, rows))
    middle = offsets.pop(len(offsets) // 2) if offsets else 0
    first, second = offsets[0::2], offsets[1::2]

    def sum_apply(total, part, inverse, hold):
        fulls = [move(total, lambda z, q: (z ^ (b if q % 2 else a), q)) for a, b in zip(first, second)]
        halves = [move(part, lambda z, q: (z ^ middle, q))] if middle else []
        return gather_apply(odd, total, fulls, halves, inverse, hold)

    def add_cores(value):
        return value + swap_core(value)

    half = length // 2
    blocks = panel.reshape(steps, depth * length // LANES, LANES)
    blocks = pltpu.with_memory_space_constraint(blocks, pltpu.HBM)
    inverse_blocks = pltpu.with_memory_space_constraint(inverse_blocks, pltpu.HBM)
    heads = pltpu.with_memory_space_constraint(right_side.reshape(count * length // LANES, LANES), pltpu.HBM)

    def across(value, bit):
        return move(value, lambda z, q: (z, q ^ bit))

    def from_chip(value, source):
        kept = value
        for bit in range(cols - 2, 0, -2):
            moved = move(value, lambda z, q: (z, q ^ bit), (source & ~1, source | 1))
            kept = jnp.where(((col ^ source) & ~1) == bit, moved, kept)
        return kept

    def on_right(here, moved):
        return jnp.where(is_right, moved, here)

    keep = jnp.where(row == 0, 1, 0).astype(jnp.int32).reshape(1)
    own_piece, start_value, block_0 = first_step(keep, heads, inverse_blocks, blocks, count)
    x_0 = jnp.where(is_odd, swap_core(own_piece), own_piece)

    def on_chip(total, step):
        total = jnp.where(is_odd == (step % 2 == 1), total, swap_core(total))
        return total, lax.dynamic_slice_in_dim(total, odd * half, half, 1)

    total, part = on_chip(update([x_0], start_value, [block_0]), 1)
    moved = across(after(total, x_0), 2)
    (inverse,) = load(moved, [(inverse_blocks, (1,))])
    piece = sum_apply(total, part, inverse, [moved])
    x_0 = on_right(x_0, moved)
    (block_1,) = load(piece, [(blocks, (1,))])
    x_1 = add_cores(piece)
    x_1 = on_right(x_1, across(x_1, 2))

    own_total = update([x_0, x_1], start_value, [block_0, block_1])
    total, part = on_chip(own_total, 2)
    first_two = after(total, jnp.concatenate([x_0, x_1], axis=1))
    moved = across(first_two, 4)
    (inverse,) = load(moved, [(inverse_blocks, (2,))])
    piece = sum_apply(total, part, inverse, [moved])
    first_two = jnp.where((col & 4) != 0, moved, first_two)
    first_two = spread(first_two, 0, bits[2:])
    (block_2,) = load(piece, [(blocks, (2,))])
    x_2 = add_cores(piece)

    total, part = on_chip(update([x_2], own_total, [block_2]), 3)
    moved = across(after(total, x_2), 2)
    x_0, x_1 = first_two[:, :depth], first_two[:, depth:]
    accum = update_from(total, [x_0, x_1], start_value, blocks, [0, 1])
    (inverse,) = load(accum, [(inverse_blocks, (3,))])
    piece = sum_apply(total, part, inverse, [moved])
    x_2 = spread(jnp.where(is_right, x_2, moved), 2, bits[1:])
    block_2, block_3 = load(piece, [(blocks, (2, 3))])
    x_3 = from_chip(add_cores(piece), 3)
    accum = update([x_2], accum, [block_2])
    accum = update([x_3], accum, [block_3])

    size = length // rows
    chunk = lambda at: lax.dynamic_slice_in_dim(accum, at * size, size, 1)
    parts = [chunk(row)]
    for offset in range(rows - 1, 0, -1):
        parts.append(move(chunk(row ^ offset), lambda z, q: (z ^ offset, q)))
    updated = add_rows(parts).reshape(count, 1, 1, size)
    return jnp.stack([x_0, x_1, x_2, x_3], axis=1), updated


def solution(mesh):
    placed = (P(None, "row", None, "col", None), P(None, "row", None), P(None, None, "col", None))
    return jax.shard_map(
        functools.partial(body, mesh.shape["row"], mesh.shape["col"]),
        mesh=mesh,
        in_specs=placed,
        out_specs=(P(None, None, "row"), P(None, None, "col", "row")),
        check_vma=False,
    )
```

```python
import functools

import jax
import jax.numpy as jnp
from jax import lax
from jax.experimental import pallas as pl
from jax.experimental.pallas import tpu as pltpu
from jax.sharding import PartitionSpec as P

LANES = 128
F32 = jnp.float32
BF16 = jnp.bfloat16
VMEM = pl.BlockSpec(memory_space=pltpu.VMEM)
SMEM = pl.BlockSpec(memory_space=pltpu.SMEM)
ANY = pl.BlockSpec(memory_space=pl.ANY)
HBM = pl.BlockSpec(memory_space=pltpu.HBM)
PARAMS = pltpu.CompilerParams(vmem_limit_bytes=12 * 2**20)


def split(value):
    head = value.astype(BF16)
    return head, (value - head.astype(F32)).astype(BF16)


def product(left, right, dims):
    count = left.shape[0]
    left_head, left_tail = split(left)
    right_head, right_tail = split(right)
    dot = functools.partial(lax.dot_general, dimension_numbers=(dims, ((), ())), preferred_element_type=F32)
    stacked = dot(jnp.concatenate([left_head, left_tail], axis=0), right_head)
    return stacked[:count] + stacked[count:] + dot(left_head, right_tail)


def columns(block_ref, first, width, rows):
    if block_ref.shape[0] == rows:
        return block_ref[:, first : first + width]
    stride = block_ref.shape[0] // rows
    parts = [block_ref[pl.ds(at // LANES, rows, stride=stride), :] for at in range(first, first + width, LANES)]
    return parts[0] if len(parts) == 1 else jnp.concatenate(parts, axis=1)


def subtract_products(solved, base_ref, block_refs, out_ref):
    length = base_ref.shape[1]
    width = 2 * LANES
    for first in range(0, length, width):
        at = slice(first, first + width)
        total = base_ref[:, at]
        for value, block_ref in zip(solved, block_refs):
            total = total - product(value, columns(block_ref, first, width, value.shape[1]), ((1,), (0,)))
        out_ref[:, at] = total


def call(kernel, outs, ins, in_specs, flops=0, scratch=(), read=0):
    moved = 4 * read + sum(4 * out.size for out in outs) if flops or read else 0
    return pl.pallas_call(
        kernel,
        out_shape=outs,
        in_specs=in_specs,
        out_specs=[VMEM] * len(outs),
        scratch_shapes=scratch,
        compiler_params=PARAMS,
        cost_estimate=pl.CostEstimate(flops=flops, bytes_accessed=moved, transcendentals=0),
    )(*ins)


def shape(*sizes):
    return jax.ShapeDtypeStruct(sizes, F32)


def start(copies):
    for copy in copies:
        copy.start()


def finish(copies):
    for copy in copies:
        copy.wait()


def first_step(keep, heads, inverse_blocks, blocks, count):
    rows, length = inverse_blocks.shape[1:]
    stride = heads.shape[0] // count
    pieces = 3
    size = length // pieces

    def kernel(keep_ref, heads_ref, inverse_ref, blocks_ref, out_ref, kept_ref, block_ref, heads_here, inverse_here, sems):
        copies = [pltpu.make_async_copy(heads_ref, heads_here, sems.at[pieces])]
        for at in range(pieces):
            piece = pl.ds(at * size, size)
            copies.append(pltpu.make_async_copy(inverse_ref.at[0, :, piece], inverse_here.at[:, piece], sems.at[at]))
        later = chunked(blocks_ref.at[0], block_ref, sems, pieces + 1)
        start(copies + later)
        copies[0].wait()
        value = columns(heads_here, 0, stride * LANES, count)
        kept_ref[...] = jnp.where(keep_ref[0] == 1, value, 0.0)
        total = jnp.zeros((count, rows), F32)
        for at in range(pieces):
            piece = slice(at * size, (at + 1) * size)
            copies[at + 1].wait()
            total = total + product(value[:, piece], inverse_here[:, piece], ((1,), (1,)))
        out_ref[...] = total
        finish(later)

    return call(
        kernel,
        [shape(count, rows), shape(count, length), shape(*blocks.shape[1:])],
        [keep, heads, inverse_blocks, blocks],
        [SMEM, HBM, HBM, HBM],
        6 * count * rows * length,
        [pltpu.VMEM(heads.shape, F32), pltpu.VMEM((rows, length), F32), pltpu.SemaphoreType.DMA((pieces + 5,))],
    )


def after(token, value):
    return lax.optimization_barrier((token, value))[1]


def chunked(source, target, sems, first, pieces=4):
    size = target.shape[0] // pieces
    parts = [pl.ds(at * size, size) for at in range(pieces)]
    return [pltpu.make_async_copy(source.at[part], target.at[part], sems.at[first + at]) for at, part in enumerate(parts)]


def load(token, arrays):
    wanted = [(at, index) for at, (_, indices) in enumerate(arrays) for index in indices]

    def kernel(token_ref, *refs):
        ins, outs, sems = refs[: len(arrays)], refs[len(arrays) : -1], refs[-1]
        copies = []
        for (at, index), out in zip(wanted, outs):
            copies += chunked(ins[at].at[index], out, sems, len(copies))
        start(copies)
        finish(copies)

    return call(
        kernel,
        [shape(*arrays[at][0].shape[1:]) for at, _ in wanted],
        [token] + [array for array, _ in arrays],
        [ANY] + [HBM] * len(arrays),
        scratch=[pltpu.SemaphoreType.DMA((4 * len(wanted),))],
    )


def update_from(token, own, solved, bases, panels, indices, read=0):
    many = len(solved)

    def kernel(own_ref, *refs):
        solved_refs, base_ref, other_base_ref, panel_ref, other_panel_ref, _, out_ref, here, sems = refs[:many], *refs[many:]

        def run(base_ref, panel_ref):
            copies = [chunked(panel_ref.at[index], here.at[at], sems, 4 * at) for at, index in enumerate(indices)]
            for copy in copies:
                start(copy)
            for copy in copies:
                finish(copy)
            subtract_products([ref[...] for ref in solved_refs], base_ref, [here.at[at] for at in range(many)], out_ref)

        pl.when(own_ref[0] == 1)(lambda: run(base_ref, panel_ref))
        pl.when(own_ref[0] != 1)(lambda: run(other_base_ref, other_panel_ref))

    return call(
        kernel,
        [shape(*bases[0].shape)],
        [own.reshape(1)] + list(solved) + list(bases) + list(panels) + [token],
        [SMEM] + [VMEM] * (many + 2) + [HBM, HBM, ANY],
        scratch=[pltpu.VMEM((many,) + panels[0].shape[1:], F32), pltpu.SemaphoreType.DMA((4 * many,))],
        read=read,
    )[0]


def load_either(token, own, panels, index, read=0):
    def kernel(token_ref, own_ref, panel_ref, other_panel_ref, out_ref, sems):
        def run(panel_ref):
            copies = chunked(panel_ref.at[index], out_ref, sems, 0)
            start(copies)
            finish(copies)

        pl.when(own_ref[0] == 1)(lambda: run(panel_ref))
        pl.when(own_ref[0] != 1)(lambda: run(other_panel_ref))

    return call(
        kernel,
        [shape(*panels[0].shape[1:])],
        [token, own.reshape(1)] + list(panels),
        [ANY, SMEM, HBM, HBM],
        scratch=[pltpu.SemaphoreType.DMA((4,))],
        read=read,
    )[0]


def update(solved, base, blocks):
    many = len(solved)

    def kernel(*refs):
        subtract_products([ref[...] for ref in refs[:many]], refs[many], refs[many + 1 : -1], refs[-1])

    flops = 6 * base.size * sum(value.shape[1] for value in solved)
    ins = list(solved) + [base] + list(blocks)
    return call(kernel, [shape(*base.shape)], ins, [VMEM] * len(ins), flops)[0]


def update_part(odd, choice, solved, base, block):
    count, length = base.shape
    half = length // 2

    def kernel(odd_ref, choice_ref, *refs):
        base_ref, block_ref, out_ref, part_ref = refs[-4:]
        value = refs[0][...]
        for at, ref in enumerate(refs[1:-4]):
            value = jnp.where(choice_ref[0] == at + 1, ref[...], value)
        subtract_products([value], base_ref, [block_ref], out_ref)
        part_ref[...] = jnp.where(odd_ref[0] == 1, out_ref[:, half:], out_ref[:, :half])

    return call(
        kernel,
        [shape(count, length), shape(count, half)],
        [odd.reshape(1), choice.reshape(1), *solved, base, block],
        [SMEM] * 2 + [VMEM] * (len(solved) + 2),
        6 * base.size * solved[0].shape[1],
    )


def add_rows(parts):
    count, length = parts[0].shape
    many = length // LANES
    if many * LANES != length:
        return sum(parts)

    def kernel(*refs):
        total = refs[0][...]
        for ref in refs[1:-1]:
            total = total + ref[...]
        for at in range(many):
            refs[-1][pl.ds(at, count, stride=many), :] = total[:, at * LANES : (at + 1) * LANES]

    return call(kernel, [shape(count * many, LANES)], parts, [VMEM] * len(parts), parts[0].size)[0]


def gather_apply(odd, own, fulls, halves, inverse, hold):
    count, length = own.shape
    rows = inverse.shape[0]

    def kernel(odd_ref, *refs):
        odd = odd_ref[0]
        own_ref, rest = refs[0], refs[1 : -2 - len(hold)]
        inverse_ref, out_ref = refs[-2 - len(hold)], refs[-1]
        value = jnp.where(odd == 1, 0.0, own_ref[...])
        for ref in rest[: len(fulls)]:
            value = value + ref[...]
        for ref in rest[len(fulls) :]:
            half = ref[...]
            zero = jnp.zeros_like(half)
            value = value + jnp.concatenate([jnp.where(odd == 1, zero, half), jnp.where(odd == 1, half, zero)], axis=1)
        out_ref[...] = product(value, inverse_ref[...], ((1,), (1,)))

    ins = [own] + fulls + halves + [inverse]
    specs = [SMEM] + [VMEM] * len(ins) + [ANY] * len(hold)
    return call(kernel, [shape(count, rows)], [odd.reshape(1)] + ins + hold, specs, 6 * own.size * rows)[0]


def body(rows, cols, panel, inverse_blocks, right_side):
    steps, depth, _, _, length = panel.shape
    count = right_side.shape[0]
    row, col = lax.axis_index("row"), lax.axis_index("col")
    odd, side = lax.rem(col, 2), lax.rem(col // 2, 2)
    is_odd, is_right = odd == 1, side == 1
    bits = [1 << at for at in range(1, cols.bit_length() - 1)]

    def move(value, target, senders=range(cols)):
        pairs = []
        for z in range(rows):
            for q in senders:
                to_z, to_q = target(z, q)
                pairs.append((z * cols + q, to_z * cols + to_q))
        return lax.ppermute(value, ("row", "col"), pairs)

    def swap_core(value):
        return move(value, lambda z, q: (z, q ^ 1))

    def spread(value, source, bits):
        for bit in bits:
            moved = move(value, lambda z, q: (z, q ^ bit))
            value = jnp.where(((col ^ source) & bit) != 0, moved, value)
        return value

    offsets = list(range(1, rows))
    middle = offsets.pop(len(offsets) // 2) if offsets else 0
    first, second = offsets[0::2], offsets[1::2]

    def sum_apply(total, part, inverse, hold):
        fulls = [move(total, lambda z, q: (z ^ (b if q % 2 else a), q)) for a, b in zip(first, second)]
        halves = [move(part, lambda z, q: (z ^ middle, q))] if middle else []
        return gather_apply(odd, total, fulls, halves, inverse, hold)

    def add_cores(value):
        return value + swap_core(value)

    half = length // 2
    blocks = panel.reshape(steps, depth * length // LANES, LANES)
    blocks = pltpu.with_memory_space_constraint(blocks, pltpu.HBM)
    inverse_blocks = pltpu.with_memory_space_constraint(inverse_blocks, pltpu.HBM)
    heads = pltpu.with_memory_space_constraint(right_side.reshape(count * length // LANES, LANES), pltpu.HBM)

    def across(value, bit):
        return move(value, lambda z, q: (z, q ^ bit))

    def from_chip(value, source):
        kept = value
        for bit in range(cols - 2, 0, -2):
            moved = move(value, lambda z, q: (z, q ^ bit), (source & ~1, source | 1))
            kept = jnp.where(((col ^ source) & ~1) == bit, moved, kept)
        return kept

    def on_right(here, moved):
        return jnp.where(is_right, moved, here)

    keep = jnp.where(row == 0, 1, 0).astype(jnp.int32).reshape(1)
    own_piece, start_value, block_0 = first_step(keep, heads, inverse_blocks, blocks, count)
    x_0 = jnp.where(is_odd, swap_core(own_piece), own_piece)

    def on_chip(total, step):
        total = jnp.where(is_odd == (step % 2 == 1), total, swap_core(total))
        return total, lax.dynamic_slice_in_dim(total, odd * half, half, 1)

    even = 1 - odd

    starts = [start_value, swap_core(after(x_0, start_value))]
    even = 1 - odd
    total, part = on_chip(update([x_0], start_value, [block_0]), 1)
    panels = [blocks, pltpu.with_memory_space_constraint(swap_core(after(total, panel.reshape(blocks.shape))), pltpu.HBM)]
    moved = across(after(total, x_0), 2)
    (inverse,) = load(moved, [(inverse_blocks, (1,))])
    piece = sum_apply(total, part, inverse, [moved])
    x_0 = on_right(x_0, moved)
    block = load_either(piece, even, panels, 1, blocks.size)
    base = update_from(piece, even, [x_0], starts, panels, [0], blocks.size)
    x_1 = add_cores(piece)
    moved = across(x_1, 2)

    total, part = update_part(odd, side, [x_1, moved], base, block)
    x_1 = on_right(x_1, moved)
    base = update_from(total, odd, [x_0, x_1], starts, panels, [0, 1])
    moved = [across(after(total, x), 4) for x in (x_0, x_1)]
    (inverse,) = load(moved[1], [(inverse_blocks, (2,))])
    piece = sum_apply(total, part, inverse, [base] + moved)
    block = load_either(piece, odd, panels, 2, blocks.size)
    x_0, x_1 = [spread(jnp.where((col & 4) != 0, far, x), 0, bits[2:]) for x, far in zip((x_0, x_1), moved)]
    x_2 = add_cores(piece)

    total, part = update_part(odd, side, [x_2], base, block)
    moved = across(after(total, x_2), 2)
    accum = update_from(total, jnp.ones_like(odd), [x_0, x_1], starts, panels, [0, 1])
    (inverse,) = load(accum, [(inverse_blocks, (3,))])
    piece = sum_apply(total, part, inverse, [moved])
    x_2 = spread(jnp.where(is_right, x_2, moved), 2, bits[1:])
    block_2, block_3 = load(piece, [(blocks, (2, 3))])
    x_3 = from_chip(add_cores(piece), 3)
    accum = update([x_2], accum, [block_2])
    accum = update([x_3], accum, [block_3])

    size = length // rows
    chunk = lambda at: lax.dynamic_slice_in_dim(accum, at * size, size, 1)
    parts = [chunk(row)]
    for offset in range(rows - 1, 0, -1):
        parts.append(move(chunk(row ^ offset), lambda z, q: (z ^ offset, q)))
    updated = add_rows(parts).reshape(count, 1, 1, size)
    return jnp.stack([x_0, x_1, x_2, x_3], axis=1), updated


def solution(mesh):
    placed = (P(None, "row", None, "col", None), P(None, "row", None), P(None, None, "col", None))
    return jax.shard_map(
        functools.partial(body, mesh.shape["row"], mesh.shape["col"]),
        mesh=mesh,
        in_specs=placed,
        out_specs=(P(None, None, "row"), P(None, None, "col", "row")),
        check_vma=False,
    )
```

```python
import functools

import jax
import jax.numpy as jnp
from jax import lax
from jax.experimental import pallas as pl
from jax.experimental.pallas import tpu as pltpu
from jax.sharding import PartitionSpec as P

LANES = 128
F32 = jnp.float32
BF16 = jnp.bfloat16
VMEM = pl.BlockSpec(memory_space=pltpu.VMEM)
SMEM = pl.BlockSpec(memory_space=pltpu.SMEM)
ANY = pl.BlockSpec(memory_space=pl.ANY)
HBM = pl.BlockSpec(memory_space=pltpu.HBM)
PARAMS = pltpu.CompilerParams(vmem_limit_bytes=12 * 2**20)


def split(value):
    head = value.astype(BF16)
    return head, (value - head.astype(F32)).astype(BF16)


def product_split(left, right_head, right_tail, dims):
    count = left.shape[0]
    left_head, left_tail = split(left)
    dot = functools.partial(lax.dot_general, dimension_numbers=(dims, ((), ())), preferred_element_type=F32)
    stacked = dot(jnp.concatenate([left_head, left_tail], axis=0), right_head)
    return stacked[:count] + stacked[count:] + dot(left_head, right_tail)


def product(left, right, dims):
    return product_split(left, *split(right), dims)


def columns(block_ref, first, width, rows):
    if block_ref.shape[0] == rows:
        return block_ref[:, first : first + width]
    stride = block_ref.shape[0] // rows
    parts = [block_ref[pl.ds(at // LANES, rows, stride=stride), :] for at in range(first, first + width, LANES)]
    return parts[0] if len(parts) == 1 else jnp.concatenate(parts, axis=1)


def subtract_products(solved, base_ref, block_refs, out_ref):
    length = base_ref.shape[1]
    width = 2 * LANES
    for first in range(0, length, width):
        at = slice(first, first + width)
        total = base_ref[:, at]
        for value, block_ref in zip(solved, block_refs):
            total = total - product(value, columns(block_ref, first, width, value.shape[1]), ((1,), (0,)))
        out_ref[:, at] = total


def call(kernel, outs, ins, in_specs, flops=0, scratch=(), read=0):
    moved = 4 * read + sum(4 * out.size for out in outs) if flops or read else 0
    return pl.pallas_call(
        kernel,
        out_shape=outs,
        in_specs=in_specs,
        out_specs=[VMEM] * len(outs),
        scratch_shapes=scratch,
        compiler_params=PARAMS,
        cost_estimate=pl.CostEstimate(flops=flops, bytes_accessed=moved, transcendentals=0),
    )(*ins)


def shape(*sizes):
    return jax.ShapeDtypeStruct(sizes, F32)


def start(copies):
    for copy in copies:
        copy.start()


def finish(copies):
    for copy in copies:
        copy.wait()


def first_step(keep, heads, inverse_blocks, blocks, count):
    rows, length = inverse_blocks.shape[1:]
    stride = heads.shape[0] // count
    pieces = 3
    size = length // pieces

    def kernel(keep_ref, heads_ref, inverse_ref, blocks_ref, out_ref, kept_ref, block_ref, heads_here, inverse_here, sems):
        copies = [pltpu.make_async_copy(heads_ref, heads_here, sems.at[pieces])]
        for at in range(pieces):
            piece = pl.ds(at * size, size)
            copies.append(pltpu.make_async_copy(inverse_ref.at[0, :, piece], inverse_here.at[:, piece], sems.at[at]))
        later = chunked(blocks_ref.at[0], block_ref, sems, pieces + 1)
        start(copies + later)
        copies[0].wait()
        value = columns(heads_here, 0, stride * LANES, count)
        kept_ref[...] = jnp.where(keep_ref[0] == 1, value, 0.0)
        total = jnp.zeros((count, rows), F32)
        for at in range(pieces):
            piece = slice(at * size, (at + 1) * size)
            copies[at + 1].wait()
            total = total + product(value[:, piece], inverse_here[:, piece], ((1,), (1,)))
        out_ref[...] = total
        finish(later)

    return call(
        kernel,
        [shape(count, rows), shape(count, length), shape(*blocks.shape[1:])],
        [keep, heads, inverse_blocks, blocks],
        [SMEM, HBM, HBM, HBM],
        6 * count * rows * length,
        [pltpu.VMEM(heads.shape, F32), pltpu.VMEM((rows, length), F32), pltpu.SemaphoreType.DMA((pieces + 5,))],
    )


def after(token, value):
    return lax.optimization_barrier((token, value))[1]


def chunked(source, target, sems, first, pieces=4):
    size = target.shape[0] // pieces
    parts = [pl.ds(at * size, size) for at in range(pieces)]
    return [pltpu.make_async_copy(source.at[part], target.at[part], sems.at[first + at]) for at, part in enumerate(parts)]


def load_inverse(token, inverse_blocks, index):
    rows, length = inverse_blocks.shape[1:]
    pieces = rows // LANES if rows % LANES == 0 else 1
    size = rows // pieces

    def kernel(token_ref, inverse_ref, head_ref, tail_ref, here, sems):
        copies = chunked(inverse_ref.at[index], here, sems, 0, pieces)
        start(copies)
        for at, copy in enumerate(copies):
            copy.wait()
            part = slice(at * size, (at + 1) * size)
            head_ref[:, part], tail_ref[:, part] = split(here[part, :].T)

    return call(
        kernel,
        [jax.ShapeDtypeStruct((length, rows), BF16)] * 2,
        [token, inverse_blocks],
        [ANY, HBM],
        scratch=[pltpu.VMEM((rows, length), F32), pltpu.SemaphoreType.DMA((pieces,))],
    )


def load(token, arrays):
    wanted = [(at, index) for at, (_, indices) in enumerate(arrays) for index in indices]

    def kernel(token_ref, *refs):
        ins, outs, sems = refs[: len(arrays)], refs[len(arrays) : -1], refs[-1]
        copies = []
        for (at, index), out in zip(wanted, outs):
            copies += chunked(ins[at].at[index], out, sems, len(copies))
        start(copies)
        finish(copies)

    return call(
        kernel,
        [shape(*arrays[at][0].shape[1:]) for at, _ in wanted],
        [token] + [array for array, _ in arrays],
        [ANY] + [HBM] * len(arrays),
        scratch=[pltpu.SemaphoreType.DMA((4 * len(wanted),))],
    )


def update_from(token, own, solved, bases, panels, indices, read=0):
    many = len(solved)

    def kernel(own_ref, *refs):
        solved_refs, base_ref, other_base_ref, panel_ref, other_panel_ref, _, out_ref, here, sems = refs[:many], *refs[many:]

        def run(base_ref, panel_ref):
            copies = [chunked(panel_ref.at[index], here.at[at], sems, 4 * at) for at, index in enumerate(indices)]
            for copy in copies:
                start(copy)
            for copy in copies:
                finish(copy)
            subtract_products([ref[...] for ref in solved_refs], base_ref, [here.at[at] for at in range(many)], out_ref)

        def skip():
            out_ref[...] = jnp.zeros_like(out_ref)

        pl.when(own_ref[0] == 1)(lambda: run(base_ref, panel_ref))
        pl.when(own_ref[0] == 0)(lambda: run(other_base_ref, other_panel_ref))
        pl.when(own_ref[0] > 1)(skip)

    return call(
        kernel,
        [shape(*bases[0].shape)],
        [own.reshape(1)] + list(solved) + list(bases) + list(panels) + [token],
        [SMEM] + [VMEM] * (many + 2) + [HBM, HBM, ANY],
        scratch=[pltpu.VMEM((many,) + panels[0].shape[1:], F32), pltpu.SemaphoreType.DMA((4 * many,))],
        read=read,
    )[0]


def load_either(token, own, panels, index, read=0):
    def kernel(token_ref, own_ref, panel_ref, other_panel_ref, out_ref, sems):
        def run(panel_ref):
            copies = chunked(panel_ref.at[index], out_ref, sems, 0)
            start(copies)
            finish(copies)

        def skip():
            out_ref[...] = jnp.zeros_like(out_ref)

        pl.when(own_ref[0] == 1)(lambda: run(panel_ref))
        pl.when(own_ref[0] == 0)(lambda: run(other_panel_ref))
        pl.when(own_ref[0] > 1)(skip)

    return call(
        kernel,
        [shape(*panels[0].shape[1:])],
        [token, own.reshape(1)] + list(panels),
        [ANY, SMEM, HBM, HBM],
        scratch=[pltpu.SemaphoreType.DMA((4,))],
        read=read,
    )[0]


def update(solved, base, blocks):
    many = len(solved)

    def kernel(*refs):
        subtract_products([ref[...] for ref in refs[:many]], refs[many], refs[many + 1 : -1], refs[-1])

    flops = 6 * base.size * sum(value.shape[1] for value in solved)
    ins = list(solved) + [base] + list(blocks)
    return call(kernel, [shape(*base.shape)], ins, [VMEM] * len(ins), flops)[0]


def update_part(odd, choice, solved, base, block):
    count, length = base.shape
    half = length // 2

    def kernel(odd_ref, choice_ref, *refs):
        base_ref, block_ref, out_ref, part_ref = refs[-4:]
        value = refs[0][...]
        for at, ref in enumerate(refs[1:-4]):
            value = jnp.where(choice_ref[0] == at + 1, ref[...], value)
        subtract_products([value], base_ref, [block_ref], out_ref)
        part_ref[...] = jnp.where(odd_ref[0] == 1, out_ref[:, half:], out_ref[:, :half])

    return call(
        kernel,
        [shape(count, length), shape(count, half)],
        [odd.reshape(1), choice.reshape(1), *solved, base, block],
        [SMEM] * 2 + [VMEM] * (len(solved) + 2),
        6 * base.size * solved[0].shape[1],
    )


def add_rows(parts):
    count, length = parts[0].shape
    many = length // LANES
    if many * LANES != length:
        return sum(parts)

    def kernel(*refs):
        total = refs[0][...]
        for ref in refs[1:-1]:
            total = total + ref[...]
        for at in range(many):
            refs[-1][pl.ds(at, count, stride=many), :] = total[:, at * LANES : (at + 1) * LANES]

    return call(kernel, [shape(count * many, LANES)], parts, [VMEM] * len(parts), parts[0].size)[0]


def gather_apply(odd, own, fulls, halves, inverse, hold):
    count, length = own.shape
    rows = inverse[0].shape[1]

    def kernel(odd_ref, *refs):
        odd = odd_ref[0]
        own_ref, rest = refs[0], refs[1 : -3 - len(hold)]
        head_ref, tail_ref = refs[-3 - len(hold)], refs[-2 - len(hold)]
        out_ref = refs[-1]
        value = jnp.where(odd == 1, 0.0, own_ref[...])
        for ref in rest[: len(fulls)]:
            value = value + ref[...]
        for ref in rest[len(fulls) :]:
            half = ref[...]
            zero = jnp.zeros_like(half)
            value = value + jnp.concatenate([jnp.where(odd == 1, zero, half), jnp.where(odd == 1, half, zero)], axis=1)
        out_ref[...] = product_split(value, head_ref[...], tail_ref[...], ((1,), (0,)))

    ins = [own] + fulls + halves + list(inverse)
    specs = [SMEM] + [VMEM] * len(ins) + [ANY] * len(hold)
    return call(kernel, [shape(count, rows)], [odd.reshape(1)] + ins + hold, specs, 6 * own.size * rows)[0]


def body(rows, cols, panel, inverse_blocks, right_side):
    steps, depth, _, _, length = panel.shape
    count = right_side.shape[0]
    row, col = lax.axis_index("row"), lax.axis_index("col")
    odd, side = lax.rem(col, 2), lax.rem(col // 2, 2)
    is_odd, is_right = odd == 1, side == 1
    bits = [1 << at for at in range(1, cols.bit_length() - 1)]

    def move(value, target, senders=range(cols)):
        pairs = []
        for z in range(rows):
            for q in senders:
                to_z, to_q = target(z, q)
                pairs.append((z * cols + q, to_z * cols + to_q))
        return lax.ppermute(value, ("row", "col"), pairs)

    def swap_core(value):
        return move(value, lambda z, q: (z, q ^ 1))

    def spread(value, source, bits):
        for bit in bits:
            moved = move(value, lambda z, q: (z, q ^ bit))
            value = jnp.where(((col ^ source) & bit) != 0, moved, value)
        return value

    offsets = list(range(1, rows))
    middle = offsets.pop(len(offsets) // 2) if offsets else 0
    first, second = offsets[0::2], offsets[1::2]

    def sum_apply(total, part, inverse, hold):
        fulls = [move(total, lambda z, q: (z ^ (b if q % 2 else a), q)) for a, b in zip(first, second)]
        halves = [move(part, lambda z, q: (z ^ middle, q))] if middle else []
        return gather_apply(odd, total, fulls, halves, inverse, hold)

    def add_cores(value):
        return value + swap_core(value)

    half = length // 2
    blocks = panel.reshape(steps, depth * length // LANES, LANES)
    blocks = pltpu.with_memory_space_constraint(blocks, pltpu.HBM)
    inverse_blocks = pltpu.with_memory_space_constraint(inverse_blocks, pltpu.HBM)
    heads = pltpu.with_memory_space_constraint(right_side.reshape(count * length // LANES, LANES), pltpu.HBM)

    def across(value, bit):
        return move(value, lambda z, q: (z, q ^ bit))

    def from_chip(value, source):
        kept = value
        for bit in range(cols - 2, 0, -2):
            moved = move(value, lambda z, q: (z, q ^ bit), (source & ~1, source | 1))
            kept = jnp.where(((col ^ source) & ~1) == bit, moved, kept)
        return kept

    def on_right(here, moved):
        return jnp.where(is_right, moved, here)

    keep = jnp.where(row == 0, 1, 0).astype(jnp.int32).reshape(1)
    own_piece, start_value, block_0 = first_step(keep, heads, inverse_blocks, blocks, count)
    x_0 = jnp.where(is_odd, swap_core(own_piece), own_piece)

    def on_chip(total, step):
        total = jnp.where(is_odd == (step % 2 == 1), total, swap_core(total))
        return total, lax.dynamic_slice_in_dim(total, odd * half, half, 1)

    even_2, odd_2 = [jnp.where(col // 2 == 1, value, 2) for value in (1 - odd, odd)]

    starts = [start_value, swap_core(after(x_0, start_value))]
    even_2, odd_2 = [jnp.where(col // 2 == 1, value, 2) for value in (1 - odd, odd)]
    total, part = on_chip(update([x_0], start_value, [block_0]), 1)
    panels = [blocks, pltpu.with_memory_space_constraint(swap_core(after(total, panel.reshape(blocks.shape))), pltpu.HBM)]
    moved = across(after(total, x_0), 2)
    inverse = load_inverse(moved, inverse_blocks, 1)
    piece = sum_apply(total, part, inverse, [moved])
    x_0 = on_right(x_0, moved)
    block = load_either(piece, even_2, panels, 1, blocks.size)
    base = update_from(piece, even_2, [x_0], starts, panels, [0], blocks.size)
    x_1 = add_cores(piece)
    moved = across(x_1, 2)

    total, part = update_part(odd, side, [x_1, moved], base, block)
    x_1 = on_right(x_1, moved)
    base = update_from(total, odd_2, [x_0, x_1], starts, panels, [0, 1])
    moved = [across(after(total, x), 4) for x in (x_0, x_1)]
    inverse = load_inverse(moved[1], inverse_blocks, 2)
    piece = sum_apply(total, part, inverse, [base] + moved)
    block = load_either(piece, odd_2, panels, 2, blocks.size)
    x_0, x_1 = [spread(jnp.where((col & 4) != 0, far, x), 0, bits[2:]) for x, far in zip((x_0, x_1), moved)]
    x_2 = add_cores(piece)

    total, part = update_part(odd, side, [x_2], base, block)
    moved = across(after(total, x_2), 2)
    accum = update_from(total, jnp.ones_like(odd), [x_0, x_1], starts, panels, [0, 1])
    inverse = load_inverse(accum, inverse_blocks, 3)
    piece = sum_apply(total, part, inverse, [moved])
    x_2 = spread(jnp.where(is_right, x_2, moved), 2, bits[1:])
    block_2, block_3 = load(piece, [(blocks, (2, 3))])
    x_3 = from_chip(add_cores(piece), 3)
    accum = update([x_2], accum, [block_2])
    accum = update([x_3], accum, [block_3])

    size = length // rows
    chunk = lambda at: lax.dynamic_slice_in_dim(accum, at * size, size, 1)
    parts = [chunk(row)]
    for offset in range(rows - 1, 0, -1):
        parts.append(move(chunk(row ^ offset), lambda z, q: (z ^ offset, q)))
    updated = add_rows(parts).reshape(count, 1, 1, size)
    return jnp.stack([x_0, x_1, x_2, x_3], axis=1), updated


def solution(mesh):
    placed = (P(None, "row", None, "col", None), P(None, "row", None), P(None, None, "col", None))
    return jax.shard_map(
        functools.partial(body, mesh.shape["row"], mesh.shape["col"]),
        mesh=mesh,
        in_specs=placed,
        out_specs=(P(None, None, "row"), P(None, None, "col", "row")),
        check_vma=False,
    )
```

```python
import functools

import jax
import jax.numpy as jnp
from jax import lax
from jax.experimental import pallas as pl
from jax.experimental.pallas import tpu as pltpu
from jax.sharding import PartitionSpec as P

LANES = 128
F32 = jnp.float32
BF16 = jnp.bfloat16
VMEM = pl.BlockSpec(memory_space=pltpu.VMEM)
SMEM = pl.BlockSpec(memory_space=pltpu.SMEM)
ANY = pl.BlockSpec(memory_space=pl.ANY)
HBM = pl.BlockSpec(memory_space=pltpu.HBM)
PARAMS = pltpu.CompilerParams(vmem_limit_bytes=12 * 2**20)


def split(value):
    head = value.astype(BF16)
    return head, (value - head.astype(F32)).astype(BF16)


def product_split(left, right_head, right_tail, dims):
    count = left.shape[0]
    left_head, left_tail = split(left)
    dot = functools.partial(lax.dot_general, dimension_numbers=(dims, ((), ())), preferred_element_type=F32)
    stacked = dot(jnp.concatenate([left_head, left_tail], axis=0), right_head)
    return stacked[:count] + stacked[count:] + dot(left_head, right_tail)


def product(left, right, dims):
    return product_split(left, *split(right), dims)


def columns(block_ref, first, width, rows):
    if block_ref.shape[0] == rows:
        return block_ref[:, first : first + width]
    stride = block_ref.shape[0] // rows
    parts = [block_ref[pl.ds(at // LANES, rows, stride=stride), :] for at in range(first, first + width, LANES)]
    return parts[0] if len(parts) == 1 else jnp.concatenate(parts, axis=1)


def subtract_products(solved, base_ref, block_refs, out_ref):
    length = base_ref.shape[1]
    width = 2 * LANES
    for first in range(0, length, width):
        at = slice(first, first + width)
        total = base_ref[:, at]
        for value, block_ref in zip(solved, block_refs):
            total = total - product(value, columns(block_ref, first, width, value.shape[1]), ((1,), (0,)))
        out_ref[:, at] = total


def call(kernel, outs, ins, in_specs, flops=0, scratch=(), read=0):
    moved = 4 * read + sum(4 * out.size for out in outs) if flops or read else 0
    return pl.pallas_call(
        kernel,
        out_shape=outs,
        in_specs=in_specs,
        out_specs=[VMEM] * len(outs),
        scratch_shapes=scratch,
        compiler_params=PARAMS,
        cost_estimate=pl.CostEstimate(flops=flops, bytes_accessed=moved, transcendentals=0),
    )(*ins)


def shape(*sizes):
    return jax.ShapeDtypeStruct(sizes, F32)


def start(copies):
    for copy in copies:
        copy.start()


def finish(copies):
    for copy in copies:
        copy.wait()


def first_step(keep, heads, inverse_blocks, blocks, count):
    rows, length = inverse_blocks.shape[1:]
    stride = heads.shape[0] // count
    pieces = 3
    size = length // pieces

    def kernel(keep_ref, heads_ref, inverse_ref, blocks_ref, out_ref, kept_ref, block_ref, heads_here, inverse_here, sems):
        copies = [pltpu.make_async_copy(heads_ref, heads_here, sems.at[pieces])]
        for at in range(pieces):
            piece = pl.ds(at * size, size)
            copies.append(pltpu.make_async_copy(inverse_ref.at[0, :, piece], inverse_here.at[:, piece], sems.at[at]))
        later = chunked(blocks_ref.at[0], block_ref, sems, pieces + 1)
        start(copies + later)
        copies[0].wait()
        value = columns(heads_here, 0, stride * LANES, count)
        kept_ref[...] = jnp.where(keep_ref[0] == 1, value, 0.0)
        total = jnp.zeros((count, rows), F32)
        for at in range(pieces):
            piece = slice(at * size, (at + 1) * size)
            copies[at + 1].wait()
            total = total + product(value[:, piece], inverse_here[:, piece], ((1,), (1,)))
        out_ref[...] = total
        finish(later)

    return call(
        kernel,
        [shape(count, rows), shape(count, length), shape(*blocks.shape[1:])],
        [keep, heads, inverse_blocks, blocks],
        [SMEM, HBM, HBM, HBM],
        6 * count * rows * length,
        [pltpu.VMEM(heads.shape, F32), pltpu.VMEM((rows, length), F32), pltpu.SemaphoreType.DMA((pieces + 5,))],
    )


def after(token, value):
    return lax.optimization_barrier((token, value))[1]


def chunked(source, target, sems, first, pieces=4):
    size = target.shape[0] // pieces
    parts = [pl.ds(at * size, size) for at in range(pieces)]
    return [pltpu.make_async_copy(source.at[part], target.at[part], sems.at[first + at]) for at, part in enumerate(parts)]


def load_inverse(token, inverse_blocks, index):
    rows, length = inverse_blocks.shape[1:]
    pieces = rows // LANES if rows % LANES == 0 else 1
    size = rows // pieces

    def kernel(token_ref, inverse_ref, head_ref, tail_ref, here, sems):
        copies = chunked(inverse_ref.at[index], here, sems, 0, pieces)
        start(copies)
        for at, copy in enumerate(copies):
            copy.wait()
            part = slice(at * size, (at + 1) * size)
            head_ref[:, part], tail_ref[:, part] = split(here[part, :].T)

    return call(
        kernel,
        [jax.ShapeDtypeStruct((length, rows), BF16)] * 2,
        [token, inverse_blocks],
        [ANY, HBM],
        scratch=[pltpu.VMEM((rows, length), F32), pltpu.SemaphoreType.DMA((pieces,))],
    )


def load(token, arrays):
    wanted = [(at, index) for at, (_, indices) in enumerate(arrays) for index in indices]

    def kernel(token_ref, *refs):
        ins, outs, sems = refs[: len(arrays)], refs[len(arrays) : -1], refs[-1]
        copies = []
        for (at, index), out in zip(wanted, outs):
            copies += chunked(ins[at].at[index], out, sems, len(copies))
        start(copies)
        finish(copies)

    return call(
        kernel,
        [shape(*arrays[at][0].shape[1:]) for at, _ in wanted],
        [token] + [array for array, _ in arrays],
        [ANY] + [HBM] * len(arrays),
        scratch=[pltpu.SemaphoreType.DMA((4 * len(wanted),))],
    )


def update_from(token, own, solved, bases, panels, indices, read=0):
    many = len(solved)

    def kernel(own_ref, *refs):
        solved_refs, base_ref, other_base_ref, panel_ref, other_panel_ref, _, out_ref, here, sems = refs[:many], *refs[many:]

        def run(base_ref, panel_ref):
            copies = [chunked(panel_ref.at[index], here.at[at], sems, 4 * at) for at, index in enumerate(indices)]
            for copy in copies:
                start(copy)
            for copy in copies:
                finish(copy)
            subtract_products([ref[...] for ref in solved_refs], base_ref, [here.at[at] for at in range(many)], out_ref)

        def skip():
            out_ref[...] = base_ref[...]

        pl.when(own_ref[0] == 1)(lambda: run(base_ref, panel_ref))
        pl.when(own_ref[0] == 0)(lambda: run(other_base_ref, other_panel_ref))
        pl.when(own_ref[0] > 1)(skip)

    return call(
        kernel,
        [shape(*bases[0].shape)],
        [own.reshape(1)] + list(solved) + list(bases) + list(panels) + [token],
        [SMEM] + [VMEM] * (many + 2) + [HBM, HBM, ANY],
        scratch=[pltpu.VMEM((many,) + panels[0].shape[1:], F32), pltpu.SemaphoreType.DMA((4 * many,))],
        read=read,
    )[0]


def load_either(token, own, panels, index, read=0):
    def kernel(token_ref, own_ref, panel_ref, other_panel_ref, out_ref, sems):
        def run(panel_ref):
            copies = chunked(panel_ref.at[index], out_ref, sems, 0)
            start(copies)
            finish(copies)

        def skip():
            out_ref[...] = jnp.zeros_like(out_ref)

        pl.when(own_ref[0] == 1)(lambda: run(panel_ref))
        pl.when(own_ref[0] == 0)(lambda: run(other_panel_ref))
        pl.when(own_ref[0] > 1)(skip)

    return call(
        kernel,
        [shape(*panels[0].shape[1:])],
        [token, own.reshape(1)] + list(panels),
        [ANY, SMEM, HBM, HBM],
        scratch=[pltpu.SemaphoreType.DMA((4,))],
        read=read,
    )[0]


def update(solved, base, blocks):
    many = len(solved)

    def kernel(*refs):
        subtract_products([ref[...] for ref in refs[:many]], refs[many], refs[many + 1 : -1], refs[-1])

    flops = 6 * base.size * sum(value.shape[1] for value in solved)
    ins = list(solved) + [base] + list(blocks)
    return call(kernel, [shape(*base.shape)], ins, [VMEM] * len(ins), flops)[0]


def update_part(odd, choice, solved, base, block):
    count, length = base.shape
    half = length // 2

    def kernel(odd_ref, choice_ref, *refs):
        base_ref, block_ref, out_ref, part_ref = refs[-4:]
        value = refs[0][...]
        for at, ref in enumerate(refs[1:-4]):
            value = jnp.where(choice_ref[0] == at + 1, ref[...], value)
        subtract_products([value], base_ref, [block_ref], out_ref)
        part_ref[...] = jnp.where(odd_ref[0] == 1, out_ref[:, half:], out_ref[:, :half])

    return call(
        kernel,
        [shape(count, length), shape(count, half)],
        [odd.reshape(1), choice.reshape(1), *solved, base, block],
        [SMEM] * 2 + [VMEM] * (len(solved) + 2),
        6 * base.size * solved[0].shape[1],
    )


def add_rows(parts):
    count, length = parts[0].shape
    many = length // LANES
    if many * LANES != length:
        return sum(parts)

    def kernel(*refs):
        total = refs[0][...]
        for ref in refs[1:-1]:
            total = total + ref[...]
        for at in range(many):
            refs[-1][pl.ds(at, count, stride=many), :] = total[:, at * LANES : (at + 1) * LANES]

    return call(kernel, [shape(count * many, LANES)], parts, [VMEM] * len(parts), parts[0].size)[0]


def gather_apply(odd, own, fulls, halves, inverse, hold):
    count, length = own.shape
    rows = inverse[0].shape[1]

    def kernel(odd_ref, *refs):
        odd = odd_ref[0]
        own_ref, rest = refs[0], refs[1 : -3 - len(hold)]
        head_ref, tail_ref = refs[-3 - len(hold)], refs[-2 - len(hold)]
        out_ref = refs[-1]
        value = jnp.where(odd == 1, 0.0, own_ref[...])
        for ref in rest[: len(fulls)]:
            value = value + ref[...]
        for ref in rest[len(fulls) :]:
            half = ref[...]
            zero = jnp.zeros_like(half)
            value = value + jnp.concatenate([jnp.where(odd == 1, zero, half), jnp.where(odd == 1, half, zero)], axis=1)
        out_ref[...] = product_split(value, head_ref[...], tail_ref[...], ((1,), (0,)))

    ins = [own] + fulls + halves + list(inverse)
    specs = [SMEM] + [VMEM] * len(ins) + [ANY] * len(hold)
    return call(kernel, [shape(count, rows)], [odd.reshape(1)] + ins + hold, specs, 6 * own.size * rows)[0]


def body(rows, cols, panel, inverse_blocks, right_side):
    steps, depth, _, _, length = panel.shape
    count = right_side.shape[0]
    row, col = lax.axis_index("row"), lax.axis_index("col")
    odd, side = lax.rem(col, 2), lax.rem(col // 2, 2)
    is_odd, is_right = odd == 1, side == 1
    bits = [1 << at for at in range(1, cols.bit_length() - 1)]

    def move(value, target, senders=range(cols)):
        pairs = []
        for z in range(rows):
            for q in senders:
                to_z, to_q = target(z, q)
                pairs.append((z * cols + q, to_z * cols + to_q))
        return lax.ppermute(value, ("row", "col"), pairs)

    def swap_core(value):
        return move(value, lambda z, q: (z, q ^ 1))

    def spread(value, source, bits):
        for bit in bits:
            moved = move(value, lambda z, q: (z, q ^ bit))
            value = jnp.where(((col ^ source) & bit) != 0, moved, value)
        return value

    offsets = list(range(1, rows))
    middle = offsets.pop(len(offsets) // 2) if offsets else 0
    first, second = offsets[0::2], offsets[1::2]

    def sum_apply(total, part, inverse, hold):
        fulls = [move(total, lambda z, q: (z ^ (b if q % 2 else a), q)) for a, b in zip(first, second)]
        halves = [move(part, lambda z, q: (z ^ middle, q))] if middle else []
        return gather_apply(odd, total, fulls, halves, inverse, hold)

    def add_cores(value):
        return value + swap_core(value)

    half = length // 2
    blocks = panel.reshape(steps, depth * length // LANES, LANES)
    blocks = pltpu.with_memory_space_constraint(blocks, pltpu.HBM)
    inverse_blocks = pltpu.with_memory_space_constraint(inverse_blocks, pltpu.HBM)
    heads = pltpu.with_memory_space_constraint(right_side.reshape(count * length // LANES, LANES), pltpu.HBM)

    def across(value, bit):
        return move(value, lambda z, q: (z, q ^ bit))

    def from_chip(value, source):
        kept = value
        for bit in range(cols - 2, 0, -2):
            moved = move(value, lambda z, q: (z, q ^ bit), (source & ~1, source | 1))
            kept = jnp.where(((col ^ source) & ~1) == bit, moved, kept)
        return kept

    def on_right(here, moved):
        return jnp.where(is_right, moved, here)

    keep = jnp.where(row == 0, 1, 0).astype(jnp.int32).reshape(1)
    own_piece, start_value, block_0 = first_step(keep, heads, inverse_blocks, blocks, count)
    x_0 = jnp.where(is_odd, swap_core(own_piece), own_piece)

    def on_chip(total, step):
        total = jnp.where(is_odd == (step % 2 == 1), total, swap_core(total))
        return total, lax.dynamic_slice_in_dim(total, odd * half, half, 1)

    even_2, odd_2 = [jnp.where(col // 2 == 1, value, 2) for value in (1 - odd, odd)]

    starts = [start_value, swap_core(after(x_0, start_value))]
    even_2, odd_2 = [jnp.where(col // 2 == 1, value, 2) for value in (1 - odd, odd)]
    total, part = on_chip(update([x_0], start_value, [block_0]), 1)
    panels = [blocks, pltpu.with_memory_space_constraint(swap_core(after(total, panel.reshape(blocks.shape))), pltpu.HBM)]
    moved = across(after(total, x_0), 2)
    inverse = load_inverse(moved, inverse_blocks, 1)
    piece = sum_apply(total, part, inverse, [moved])
    x_0 = on_right(x_0, moved)
    block = load_either(piece, even_2, panels, 1, blocks.size)
    base = update_from(piece, even_2, [x_0], starts, panels, [0], blocks.size)
    x_1 = add_cores(piece)
    moved = across(x_1, 2)

    total, part = update_part(odd, side, [x_1, moved], base, block)
    x_1 = on_right(x_1, moved)
    base = update_from(total, odd_2, [x_0, x_1], starts, panels, [0, 1])
    moved = [across(after(total, x), 4) for x in (x_0, x_1)]
    inverse = load_inverse(moved[1], inverse_blocks, 2)
    piece = sum_apply(total, part, inverse, [base] + moved)
    block = load_either(piece, odd_2, panels, 2, blocks.size)
    x_0, x_1 = [spread(jnp.where((col & 4) != 0, far, x), 0, bits[2:]) for x, far in zip((x_0, x_1), moved)]
    x_2 = add_cores(piece)

    total, part = update_part(odd, side, [x_2], base, block)
    moved = across(after(total, x_2), 2)
    x_2 = jnp.where(is_right, x_2, moved)
    near = col // 4 == 0
    known = [x_0, x_1, jnp.where(near, x_2, 0.0)]
    accum = update_from(moved, jnp.ones_like(odd), known, starts, panels, [0, 1, 2])
    inverse = load_inverse(accum, inverse_blocks, 3)
    piece = sum_apply(total, part, inverse, [moved])
    x_2 = spread(x_2, 2, bits[1:])
    (block_3,) = load(piece, [(blocks, (3,))])
    x_3 = from_chip(add_cores(piece), 3)
    accum = update_from(block_3, jnp.where(near, 2, 1), [x_2], [accum, accum], panels, [2])
    accum = update([x_3], accum, [block_3])

    size = length // rows
    chunk = lambda at: lax.dynamic_slice_in_dim(accum, at * size, size, 1)
    parts = [chunk(row)]
    for offset in range(rows - 1, 0, -1):
        parts.append(move(chunk(row ^ offset), lambda z, q: (z ^ offset, q)))
    updated = add_rows(parts).reshape(count, 1, 1, size)
    return jnp.stack([x_0, x_1, x_2, x_3], axis=1), updated


def solution(mesh):
    placed = (P(None, "row", None, "col", None), P(None, "row", None), P(None, None, "col", None))
    return jax.shard_map(
        functools.partial(body, mesh.shape["row"], mesh.shape["col"]),
        mesh=mesh,
        in_specs=placed,
        out_specs=(P(None, None, "row"), P(None, None, "col", "row")),
        check_vma=False,
    )
```

```python
import functools

import jax
import jax.numpy as jnp
from jax import lax
from jax.experimental import pallas as pl
from jax.experimental.pallas import tpu as pltpu
from jax.sharding import PartitionSpec as P

LANES = 128
F32 = jnp.float32
BF16 = jnp.bfloat16
VMEM = pl.BlockSpec(memory_space=pltpu.VMEM)
SMEM = pl.BlockSpec(memory_space=pltpu.SMEM)
ANY = pl.BlockSpec(memory_space=pl.ANY)
HBM = pl.BlockSpec(memory_space=pltpu.HBM)
PARAMS = pltpu.CompilerParams(vmem_limit_bytes=12 * 2**20)


def split(value):
    head = value.astype(BF16)
    return head, (value - head.astype(F32)).astype(BF16)


def product_split(left, right_head, right_tail, dims):
    count = left.shape[0]
    left_head, left_tail = split(left)
    dot = functools.partial(lax.dot_general, dimension_numbers=(dims, ((), ())), preferred_element_type=F32)
    stacked = dot(jnp.concatenate([left_head, left_tail], axis=0), right_head)
    return stacked[:count] + stacked[count:] + dot(left_head, right_tail)


def product(left, right, dims):
    return product_split(left, *split(right), dims)


def columns(block_ref, first, width, rows):
    if block_ref.shape[0] == rows:
        return block_ref[:, first : first + width]
    stride = block_ref.shape[0] // rows
    parts = [block_ref[pl.ds(at // LANES, rows, stride=stride), :] for at in range(first, first + width, LANES)]
    return parts[0] if len(parts) == 1 else jnp.concatenate(parts, axis=1)


def subtract_products(solved, base_ref, block_refs, out_ref):
    length = base_ref.shape[1]
    width = 2 * LANES
    for first in range(0, length, width):
        at = slice(first, first + width)
        total = base_ref[:, at]
        for value, block_ref in zip(solved, block_refs):
            total = total - product(value, columns(block_ref, first, width, value.shape[1]), ((1,), (0,)))
        out_ref[:, at] = total


def call(kernel, outs, ins, in_specs, flops=0, scratch=(), read=0):
    moved = 4 * read + sum(4 * out.size for out in outs) if flops or read else 0
    return pl.pallas_call(
        kernel,
        out_shape=outs,
        in_specs=in_specs,
        out_specs=[VMEM] * len(outs),
        scratch_shapes=scratch,
        compiler_params=PARAMS,
        cost_estimate=pl.CostEstimate(flops=flops, bytes_accessed=moved, transcendentals=0),
    )(*ins)


def shape(*sizes):
    return jax.ShapeDtypeStruct(sizes, F32)


def start(copies):
    for copy in copies:
        copy.start()


def finish(copies):
    for copy in copies:
        copy.wait()


def first_step(keep, heads, inverse_blocks, blocks, count):
    rows, length = inverse_blocks.shape[1:]
    stride = heads.shape[0] // count
    pieces = 3
    size = length // pieces

    def kernel(keep_ref, heads_ref, inverse_ref, blocks_ref, out_ref, kept_ref, block_ref, heads_here, inverse_here, sems):
        copies = [pltpu.make_async_copy(heads_ref, heads_here, sems.at[pieces])]
        for at in range(pieces):
            piece = pl.ds(at * size, size)
            copies.append(pltpu.make_async_copy(inverse_ref.at[0, :, piece], inverse_here.at[:, piece], sems.at[at]))
        later = chunked(blocks_ref.at[0], block_ref, sems, pieces + 1)
        start(copies + later)
        copies[0].wait()
        value = columns(heads_here, 0, stride * LANES, count)
        kept_ref[...] = jnp.where(keep_ref[0] == 1, value, 0.0)
        total = jnp.zeros((count, rows), F32)
        for at in range(pieces):
            piece = slice(at * size, (at + 1) * size)
            copies[at + 1].wait()
            total = total + product(value[:, piece], inverse_here[:, piece], ((1,), (1,)))
        out_ref[...] = total
        finish(later)

    return call(
        kernel,
        [shape(count, rows), shape(count, length), shape(*blocks.shape[1:])],
        [keep, heads, inverse_blocks, blocks],
        [SMEM, HBM, HBM, HBM],
        6 * count * rows * length,
        [pltpu.VMEM(heads.shape, F32), pltpu.VMEM((rows, length), F32), pltpu.SemaphoreType.DMA((pieces + 5,))],
    )


def after(token, value):
    return lax.optimization_barrier((token, value))[1]


def chunked(source, target, sems, first, pieces=4):
    size = target.shape[0] // pieces
    parts = [pl.ds(at * size, size) for at in range(pieces)]
    return [pltpu.make_async_copy(source.at[part], target.at[part], sems.at[first + at]) for at, part in enumerate(parts)]


def load_inverse(token, inverse_blocks, index):
    rows, length = inverse_blocks.shape[1:]
    pieces = rows // LANES if rows % LANES == 0 else 1
    size = rows // pieces

    def kernel(token_ref, inverse_ref, head_ref, tail_ref, here, sems):
        copies = chunked(inverse_ref.at[index], here, sems, 0, pieces)
        start(copies)
        for at, copy in enumerate(copies):
            copy.wait()
            part = slice(at * size, (at + 1) * size)
            head_ref[:, part], tail_ref[:, part] = split(here[part, :].T)

    return call(
        kernel,
        [jax.ShapeDtypeStruct((length, rows), BF16)] * 2,
        [token, inverse_blocks],
        [ANY, HBM],
        scratch=[pltpu.VMEM((rows, length), F32), pltpu.SemaphoreType.DMA((pieces,))],
    )


def load(token, arrays):
    wanted = [(at, index) for at, (_, indices) in enumerate(arrays) for index in indices]

    def kernel(token_ref, *refs):
        ins, outs, sems = refs[: len(arrays)], refs[len(arrays) : -1], refs[-1]
        copies = []
        for (at, index), out in zip(wanted, outs):
            copies += chunked(ins[at].at[index], out, sems, len(copies))
        start(copies)
        finish(copies)

    return call(
        kernel,
        [shape(*arrays[at][0].shape[1:]) for at, _ in wanted],
        [token] + [array for array, _ in arrays],
        [ANY] + [HBM] * len(arrays),
        scratch=[pltpu.SemaphoreType.DMA((4 * len(wanted),))],
    )


def update_from(token, own, solved, bases, panels, indices, read=0):
    many = len(solved)

    def kernel(own_ref, *refs):
        solved_refs, base_ref, other_base_ref, panel_ref, other_panel_ref, _, out_ref, here, sems = refs[:many], *refs[many:]

        def run(base_ref, panel_ref):
            copies = [chunked(panel_ref.at[index], here.at[at], sems, 4 * at) for at, index in enumerate(indices)]
            for copy in copies:
                start(copy)
            for copy in copies:
                finish(copy)
            subtract_products([ref[...] for ref in solved_refs], base_ref, [here.at[at] for at in range(many)], out_ref)

        def skip():
            out_ref[...] = jnp.zeros_like(out_ref)

        pl.when(own_ref[0] == 1)(lambda: run(base_ref, panel_ref))
        pl.when(own_ref[0] == 0)(lambda: run(other_base_ref, other_panel_ref))
        pl.when(own_ref[0] > 1)(skip)

    return call(
        kernel,
        [shape(*bases[0].shape)],
        [own.reshape(1)] + list(solved) + list(bases) + list(panels) + [token],
        [SMEM] + [VMEM] * (many + 2) + [HBM, HBM, ANY],
        scratch=[pltpu.VMEM((many,) + panels[0].shape[1:], F32), pltpu.SemaphoreType.DMA((4 * many,))],
        read=read,
    )[0]


def load_either(token, own, panels, index, read=0):
    def kernel(token_ref, own_ref, panel_ref, other_panel_ref, out_ref, sems):
        def run(panel_ref):
            copies = chunked(panel_ref.at[index], out_ref, sems, 0)
            start(copies)
            finish(copies)

        def skip():
            out_ref[...] = jnp.zeros_like(out_ref)

        pl.when(own_ref[0] == 1)(lambda: run(panel_ref))
        pl.when(own_ref[0] == 0)(lambda: run(other_panel_ref))
        pl.when(own_ref[0] > 1)(skip)

    return call(
        kernel,
        [shape(*panels[0].shape[1:])],
        [token, own.reshape(1)] + list(panels),
        [ANY, SMEM, HBM, HBM],
        scratch=[pltpu.SemaphoreType.DMA((4,))],
        read=read,
    )[0]


def update(solved, base, blocks):
    many = len(solved)

    def kernel(*refs):
        subtract_products([ref[...] for ref in refs[:many]], refs[many], refs[many + 1 : -1], refs[-1])

    flops = 6 * base.size * sum(value.shape[1] for value in solved)
    ins = list(solved) + [base] + list(blocks)
    return call(kernel, [shape(*base.shape)], ins, [VMEM] * len(ins), flops)[0]


def update_part(odd, choice, solved, base, block):
    count, length = base.shape
    half = length // 2

    def kernel(odd_ref, choice_ref, *refs):
        base_ref, block_ref, out_ref, part_ref = refs[-4:]
        value = refs[0][...]
        for at, ref in enumerate(refs[1:-4]):
            value = jnp.where(choice_ref[0] == at + 1, ref[...], value)
        subtract_products([value], base_ref, [block_ref], out_ref)
        part_ref[...] = jnp.where(odd_ref[0] == 1, out_ref[:, half:], out_ref[:, :half])

    return call(
        kernel,
        [shape(count, length), shape(count, half)],
        [odd.reshape(1), choice.reshape(1), *solved, base, block],
        [SMEM] * 2 + [VMEM] * (len(solved) + 2),
        6 * base.size * solved[0].shape[1],
    )


def add_rows(parts):
    count, length = parts[0].shape
    many = length // LANES
    if many * LANES != length:
        return sum(parts)

    def kernel(*refs):
        total = refs[0][...]
        for ref in refs[1:-1]:
            total = total + ref[...]
        for at in range(many):
            refs[-1][pl.ds(at, count, stride=many), :] = total[:, at * LANES : (at + 1) * LANES]

    return call(kernel, [shape(count * many, LANES)], parts, [VMEM] * len(parts), parts[0].size)[0]


def gather_apply(odd, own, fulls, halves, inverse, hold):
    count, length = own.shape
    rows = inverse[0].shape[1]

    def kernel(odd_ref, *refs):
        odd = odd_ref[0]
        own_ref, rest = refs[0], refs[1 : -3 - len(hold)]
        head_ref, tail_ref = refs[-3 - len(hold)], refs[-2 - len(hold)]
        out_ref = refs[-1]
        value = jnp.where(odd == 1, 0.0, own_ref[...])
        for ref in rest[: len(fulls)]:
            value = value + ref[...]
        for ref in rest[len(fulls) :]:
            half = ref[...]
            zero = jnp.zeros_like(half)
            value = value + jnp.concatenate([jnp.where(odd == 1, zero, half), jnp.where(odd == 1, half, zero)], axis=1)
        out_ref[...] = product_split(value, head_ref[...], tail_ref[...], ((1,), (0,)))

    ins = [own] + fulls + halves + list(inverse)
    specs = [SMEM] + [VMEM] * len(ins) + [ANY] * len(hold)
    return call(kernel, [shape(count, rows)], [odd.reshape(1)] + ins + hold, specs, 6 * own.size * rows)[0]


def body(rows, cols, panel, inverse_blocks, right_side):
    steps, depth, _, _, length = panel.shape
    count = right_side.shape[0]
    row, col = lax.axis_index("row"), lax.axis_index("col")
    odd, side = lax.rem(col, 2), lax.rem(col // 2, 2)
    is_odd, is_right = odd == 1, side == 1
    bits = [1 << at for at in range(1, cols.bit_length() - 1)]

    def move(value, target, senders=range(cols)):
        pairs = []
        for z in range(rows):
            for q in senders:
                to_z, to_q = target(z, q)
                pairs.append((z * cols + q, to_z * cols + to_q))
        return lax.ppermute(value, ("row", "col"), pairs)

    def swap_core(value):
        return move(value, lambda z, q: (z, q ^ 1))

    def spread(value, source, bits):
        for bit in bits:
            moved = move(value, lambda z, q: (z, q ^ bit))
            value = jnp.where(((col ^ source) & bit) != 0, moved, value)
        return value

    offsets = list(range(1, rows))
    middle = offsets.pop(len(offsets) // 2) if offsets else 0
    first, second = offsets[0::2], offsets[1::2]

    def sum_apply(total, part, inverse, hold):
        fulls = [move(total, lambda z, q: (z ^ (b if q % 2 else a), q)) for a, b in zip(first, second)]
        halves = [move(part, lambda z, q: (z ^ middle, q))] if middle else []
        return gather_apply(odd, total, fulls, halves, inverse, hold)

    def add_cores(value):
        return value + swap_core(value)

    half = length // 2
    blocks = panel.reshape(steps, depth * length // LANES, LANES)
    blocks = pltpu.with_memory_space_constraint(blocks, pltpu.HBM)
    inverse_blocks = pltpu.with_memory_space_constraint(inverse_blocks, pltpu.HBM)
    heads = pltpu.with_memory_space_constraint(right_side.reshape(count * length // LANES, LANES), pltpu.HBM)

    def across(value, bit):
        return move(value, lambda z, q: (z, q ^ bit))

    def from_chip(value, source):
        kept = value
        for bit in range(cols - 2, 0, -2):
            moved = move(value, lambda z, q: (z, q ^ bit), (source & ~1, source | 1))
            kept = jnp.where(((col ^ source) & ~1) == bit, moved, kept)
        return kept

    def on_right(here, moved):
        return jnp.where(is_right, moved, here)

    keep = jnp.where(row == 0, 1, 0).astype(jnp.int32).reshape(1)
    own_piece, start_value, block_0 = first_step(keep, heads, inverse_blocks, blocks, count)
    x_0 = jnp.where(is_odd, swap_core(own_piece), own_piece)

    def on_chip(total, step):
        total = jnp.where(is_odd == (step % 2 == 1), total, swap_core(total))
        return total, lax.dynamic_slice_in_dim(total, odd * half, half, 1)

    even_2, odd_2 = [jnp.where(col // 2 == 1, value, 2) for value in (1 - odd, odd)]

    starts = [start_value, swap_core(after(x_0, start_value))]
    even_2, odd_2 = [jnp.where(col // 2 == 1, value, 2) for value in (1 - odd, odd)]
    total, part = on_chip(update([x_0], start_value, [block_0]), 1)
    panels = [blocks, pltpu.with_memory_space_constraint(swap_core(after(total, panel.reshape(blocks.shape))), pltpu.HBM)]
    moved = across(after(total, x_0), 2)
    inverse = load_inverse(moved, inverse_blocks, 1)
    piece = sum_apply(total, part, inverse, [moved])
    x_0 = on_right(x_0, moved)
    block = load_either(piece, even_2, panels, 1, blocks.size)
    base = update_from(piece, even_2, [x_0], starts, panels, [0], blocks.size)
    x_1 = add_cores(piece)
    moved = across(x_1, 2)

    total, part = update_part(odd, side, [x_1, moved], base, block)
    x_1 = on_right(x_1, moved)
    base = update_from(total, odd_2, [x_0, x_1], starts, panels, [0, 1])
    moved = [across(after(total, x), 4) for x in (x_0, x_1)]
    inverse = load_inverse(moved[1], inverse_blocks, 2)
    piece = sum_apply(total, part, inverse, [base] + moved)
    block = load_either(piece, odd_2, panels, 2, blocks.size)
    x_0, x_1 = [spread(jnp.where((col & 4) != 0, far, x), 0, bits[2:]) for x, far in zip((x_0, x_1), moved)]
    x_2 = add_cores(piece)

    total, part = update_part(odd, side, [x_2], base, block)
    moved = across(after(total, x_2), 2)
    accum = update_from(total, jnp.ones_like(odd), [x_0, x_1], starts, panels, [0, 1])
    inverse = load_inverse(accum, inverse_blocks, 3)
    piece = sum_apply(total, part, inverse, [moved])
    x_2 = spread(jnp.where(is_right, x_2, moved), 2, bits[1:])
    block_2, block_3 = load(piece, [(blocks, (2, 3))])
    x_3 = from_chip(add_cores(piece), 3)
    accum = update([x_2], accum, [block_2])
    accum = update([x_3], accum, [block_3])

    size = length // rows
    chunk = lambda at: lax.dynamic_slice_in_dim(accum, at * size, size, 1)
    parts = [chunk(row)]
    for offset in list(range(rows // 2, rows)) + list(range(1, rows // 2)):
        parts.append(move(chunk(row ^ offset), lambda z, q: (z ^ offset, q)))
    updated = add_rows(parts).reshape(count, 1, 1, size)
    return jnp.stack([x_0, x_1, x_2, x_3], axis=1), updated


def solution(mesh):
    placed = (P(None, "row", None, "col", None), P(None, "row", None), P(None, None, "col", None))
    return jax.shard_map(
        functools.partial(body, mesh.shape["row"], mesh.shape["col"]),
        mesh=mesh,
        in_specs=placed,
        out_specs=(P(None, None, "row"), P(None, None, "col", "row")),
        check_vma=False,
    )
```
